32 devices in a mesh: rep: 2 (over x), fsdp: 16 (over z, y, core).
Axes of the slice: x: 2, y: 2, z: 4, core: 2. Of those that a mesh axis runs over, the one named last changes fastest.
Arguments:
- inputs: bfloat16 [2, 2048, 7168], P('rep', 'fsdp'), may hold values from -6 to 6
- cotangent: bfloat16 [2, 2048, 7168], P('rep', 'fsdp'), may hold values from -6 to 6
- weights: float32 [2, 2, 3584, 128], P('rep', None, 'fsdp'), may hold values from -6 to 6
- first_moment: float32 [2, 2, 3584, 128], P('rep', None, 'fsdp'), may hold values from -0.015625 to 0.015625
- second_moment: float32 [2, 2, 3584, 128], P('rep', None, 'fsdp'), may hold values from 1e-08 to 1e-05
- anchor: float32 [3584, 128], P('fsdp'), may hold values from -6 to 6
- momentum: float32 [3584, 128], P('fsdp'), may hold values from -4 to 4
- fragment: int32 [1], replicated, may hold values from 1 to 64
Outputs:
- new_weights: float32 [2, 2, 3584, 128], P('rep', None, 'fsdp')
- new_anchor: float32 [3584, 128], P('fsdp')
- new_momentum: float32 [3584, 128], P('fsdp')
The draws below stay inside these ranges and needn't reach their ends.
All inputs are finite; a program needn't handle non-finite values.
Results may differ from the reference program's by a relative error of at most 0.0022.
Values may be sent and summed in bfloat16 or wider, within the bound.
No kernel may reach another device: no remote copies, remote signals or barrier semaphores. Data moves between devices by JAX's collectives and lax.ppermute only.
A program may use at most 64 MiB of HBM per device.

```python
import math
import jax
import jax.numpy as jnp
from jax import lax

D = 7168
H = 32
L = 2
TOK_DEV = 128
TOKENS = 2048
FLAT = 3584
N_REP = 2
N_FSDP = 16


def block_levels(key, shape, pieces, low, largest):
    level, own = 1.0, jax.random.fold_in(key, 6)
    for axis_at, parts in pieces:
        draws = jnp.exp(jax.random.uniform(jax.random.fold_in(own, axis_at), (parts,), jnp.float32, low / len(pieces), largest / len(pieces)))
        level = level * jnp.repeat(draws, shape[axis_at] // parts).reshape([-1 if axis == axis_at else 1 for axis in range(len(shape))])
    return level


def normal_values(rng, extent, width, most, shards=(), kind=jnp.bfloat16):
    drawn = jax.random.normal(rng, extent, jnp.float32) * width
    if len(shards) > 0:
        drawn = block_levels(rng, extent, shards, -0.22, 0.18) * drawn
    return jnp.clip(drawn, min=-most, max=most).astype(kind)


def setup_inputs(seed: int = 0) -> dict:
    key_of = jax.random.split(jax.random.key(seed), 9)
    return {
        "inputs": normal_values(key_of[0], (N_REP, TOKENS, D), 1.0, 6.0, ((0, 2), (1, 16))),
        "cotangent": normal_values(key_of[1], (N_REP, TOKENS, D), 1.0, 6.0, ((0, 2), (1, 16))),
        "weights": normal_values(key_of[2], (N_REP, L, FLAT, 128), 1.0, 6.0, ((0, 2), (2, 16)), jnp.float32),
        "first_moment": normal_values(key_of[3], (N_REP, L, FLAT, 128), 0.001, 0.015625, ((0, 2), (2, 16)), jnp.float32),
        "second_moment": jnp.clip(jnp.exp(math.log(9.999999747378752e-06) - 6.9077553 * jax.random.uniform(key_of[4], (N_REP, L, FLAT, 128), jnp.float32) ** block_levels(key_of[4], (N_REP, L, FLAT, 128), ((0, 2), (2, 16)), -0.2, 0.2)), 9.99999993922529e-09, 9.999999747378752e-06),
        "anchor": normal_values(key_of[5], (FLAT, 128), 1.0, 6.0, ((0, 16),), jnp.float32),
        "momentum": normal_values(key_of[6], (FLAT, 128), 0.3, 4.0, ((0, 16),), jnp.float32),
        "fragment": jax.random.randint(key_of[7], (1,), 1, 65).astype(jnp.int32),
    }


norm_eps = 1e-05
beta_one = 0.9
beta_two = 0.95
adam_eps = 1e-08
decay_rate = 0.1
inner_rate = 0.05
outer_rate = 0.7
outer_beta = 0.9
mixing = 0.5

def layer_forward(hidden_in, w_in, w_out):
    inputs_f32 = hidden_in.astype(jnp.float32)
    inv_rms = lax.rsqrt(lax.optimization_barrier(jnp.mean(inputs_f32 * inputs_f32, axis=-1, keepdims=True)) + norm_eps)
    normed = (inputs_f32 * inv_rms).astype(jnp.bfloat16)
    in_scale = w_in.shape[1] ** (-0.5)
    out_scale = w_out.shape[0] ** (-0.5)
    pre_act = lax.dot_general(normed, w_in, (((1,), (1,)), ((), ())), preferred_element_type=jnp.float32) * in_scale
    activated = jax.nn.silu(pre_act).astype(jnp.bfloat16)
    layer_out = (inputs_f32 + jnp.dot(activated, w_out, preferred_element_type=jnp.float32) * out_scale).astype(jnp.bfloat16)
    return (layer_out, (inputs_f32, inv_rms, normed, pre_act, activated))

def layer_backward(grad_out, w_in, w_out, saved, need_input):
    inputs_f32, inv_rms, normed, pre_act, activated = saved
    in_scale = w_in.shape[1] ** (-0.5)
    out_scale = w_out.shape[0] ** (-0.5)
    grad_w_out = lax.dot_general(activated, grad_out, (((0,), (0,)), ((), ())), preferred_element_type=jnp.float32) * out_scale
    grad_act = lax.dot_general(grad_out, w_out, (((1,), (1,)), ((), ())), preferred_element_type=jnp.float32) * out_scale
    sigmoid_pre = jax.nn.sigmoid(pre_act)
    grad_pre = (grad_act * sigmoid_pre * (1.0 + pre_act * (1.0 - sigmoid_pre))).astype(jnp.bfloat16)
    grad_w_in = lax.dot_general(grad_pre, normed, (((0,), (0,)), ((), ())), preferred_element_type=jnp.float32) * in_scale
    if not need_input:
        return (grad_w_in, grad_w_out, grad_out)
    grad_norm = jnp.dot(grad_pre, w_in, preferred_element_type=jnp.float32) * in_scale
    inner_sum = lax.optimization_barrier(jnp.sum(grad_norm * inputs_f32, axis=-1, keepdims=True)) / inputs_f32.shape[1]
    grad_in = grad_out.astype(jnp.float32) + inv_rms * grad_norm - inputs_f32 * (inv_rms * inv_rms * inv_rms) * inner_sum
    return (grad_w_in, grad_w_out, grad_in.astype(jnp.bfloat16))

def reference(inputs, cotangent, weights, first_moment, second_moment, anchor, momentum, fragment):
    count = fragment[0].astype(jnp.int32)
    chosen = jnp.remainder(count, L).astype(jnp.int32)
    count_real = count.astype(jnp.float32)
    correct_one = 1.0 - jnp.exp(count_real * math.log(beta_one))
    correct_two = 1.0 - jnp.exp(count_real * math.log(beta_two))
    updated_all = []
    total = jnp.zeros(anchor.shape, jnp.float32)
    for replica in range(N_REP):
        params = weights[replica]
        packed = params.astype(jnp.bfloat16).reshape(L, 2, H, D)
        current = inputs[replica]
        saved_list = []
        for layer_index in range(L):
            current, saved = layer_forward(current, packed[layer_index, 0], packed[layer_index, 1])
            saved_list.append(saved)
        upstream = cotangent[replica]
        grads = [None] * L
        for layer_index in reversed(range(L)):
            grad_w_in, grad_w_out, upstream = layer_backward(upstream, packed[layer_index, 0], packed[layer_index, 1], saved_list[layer_index], layer_index > 0)
            grads[layer_index] = jnp.stack([grad_w_in, grad_w_out]).reshape(FLAT, 128)
        gradient = jnp.stack(grads) / (TOK_DEV * N_FSDP)
        moment_one = beta_one * first_moment[replica] + (1.0 - beta_one) * gradient
        moment_two = beta_two * second_moment[replica] + (1.0 - beta_two) * gradient * gradient
        updated = params - inner_rate * (moment_one / correct_one / (jnp.sqrt(moment_two / correct_two) + adam_eps) + decay_rate * params)
        updated_all.append(updated)
        total = total + (anchor - lax.dynamic_index_in_dim(params, chosen, 0, keepdims=False))
    mean_delta = total / N_REP
    new_momentum = outer_beta * momentum + mean_delta
    new_anchor = anchor - outer_rate * (mean_delta + outer_beta * new_momentum)
    selector = (jnp.arange(L, dtype=jnp.int32) == chosen)[:, None, None]
    merged = [jnp.where(selector, mixing * upd + (1.0 - mixing) * new_anchor[None], upd) for upd in updated_all]
    return (jnp.stack(merged), new_anchor, new_momentum)
```

```python
import functools
import math

import jax
import jax.numpy as jnp
from jax import lax
from jax.experimental import pallas as pl
from jax.experimental.pallas import tpu as pltpu
from jax.sharding import PartitionSpec as P

norm_eps = 1e-05
beta_one = 0.9
beta_two = 0.95
adam_eps = 1e-08
decay_rate = 0.1
inner_rate = 0.05
outer_rate = 0.7
outer_beta = 0.9
mixing = 0.5
ROWS = 8


def swap(value, axis, mask):
    size = lax.axis_size(axis)
    return lax.ppermute(value, axis, [(i, i ^ mask) for i in range(size)])


def gather_blocks(own, axis, early):
    size = lax.axis_size(axis)
    tops = range(4, size, 4)
    have = {0: own}

    def take(k):
        have[k] = swap(have[k & (k - 1)], axis, k & -k)

    for k in tops:
        if k & (k - 1) == 0:
            take(k)
        if k == 4:
            take(2)
    take(1)
    for k in tops:
        if k in have:
            have[k], early = lax.optimization_barrier((have[k], early))
    for k in tops:
        if k not in have:
            take(k)
        take(k + 2)
    for k in range(3, size, 2):
        take(k)
    return [have[k] for k in range(size)], early


def add_f32(left, right):
    return left.astype(jnp.float32) + right.astype(jnp.float32)


def reduce_blocks(blocks, odd_sets, axis):
    size = lax.axis_size(axis)
    left = dict(blocks)
    for ks, terms in odd_sets:
        came = swap(terms, axis, 1)
        for place, k in enumerate(ks):
            left[k - 1] = add_f32(left[k - 1], came[place])
    bit = 2
    while bit < size:
        for k in sorted(left, reverse=True):
            if k & bit:
                part = left.pop(k)
                left[k ^ bit] = left[k ^ bit] + swap(part.astype(jnp.bfloat16), axis, bit).astype(jnp.float32)
        bit *= 2
    return left[0]


def output_sets(size):
    odd = list(range(size - 1, 0, -2))
    sends = [k for k in odd if k & 2]
    return [sends[:1], sends[1:], [k for k in odd if not k & 2], list(range(0, size, 2))]


def dot_nt(left, right):
    return lax.dot_general(left, right, (((1,), (1,)), ((), ())), preferred_element_type=jnp.float32)


def dot_nn(left, right):
    return jnp.dot(left, right, preferred_element_type=jnp.float32)


def adapter_kernel(n_pieces, places, units, width, *refs):
    upper_ref, normed0, h0, g2 = refs[:4]
    pieces = refs[4 : 4 + n_pieces]
    outs = refs[4 + n_pieces : -4]
    w_ref, h1, normed1, g1 = refs[-4:]
    tokens, model_width = h0.shape
    stacked = n_pieces * ROWS // 2
    hidden = stacked // 2
    in_scale = model_width ** (-0.5)
    out_scale = hidden ** (-0.5)
    steps = model_width // width
    upper = upper_ref[0]
    half = n_pieces // 2
    layer_of = (lax.broadcasted_iota(jnp.int32, (tokens, stacked), 1) % (2 * units)) // units
    zeros = jnp.zeros((tokens, stacked), jnp.float32)

    def cut(step):
        return pl.ds(pl.multiple_of(step * width, width), width)

    def first(step, carry):
        pre, grad = carry
        at = cut(step)
        for side in range(2):
            parts = [pieces[side * half + j][:, at].astype(jnp.float32) for j in range(half)]
            w_ref[side ^ upper, :, at] = jnp.concatenate(parts).astype(jnp.bfloat16)
        pre = pre + dot_nt(normed0[:, at], w_ref[0, :, at])
        grad = grad + dot_nt(g2[:, at], w_ref[1, :, at])
        return pre, grad

    pre0, grad_act1 = lax.fori_loop(0, steps, first, (zeros, zeros))
    pre0 = pre0 * in_scale
    sig0 = jax.nn.sigmoid(pre0)
    act0 = jnp.where(layer_of == 0, pre0 * sig0, 0.0)
    act0_low = act0.astype(jnp.bfloat16)

    def second(step, squares):
        at = cut(step)
        out = h0[:, at].astype(jnp.float32) + dot_nn(act0_low, w_ref[1, :, at]) * out_scale
        low = out.astype(jnp.bfloat16)
        h1[:, at] = low
        out = low.astype(jnp.float32)
        out = out * out
        for j in range(0, width, 128):
            squares = squares + out[:, j : j + 128]
        return squares

    squares = lax.fori_loop(0, steps, second, jnp.zeros((tokens, 128), jnp.float32))
    inv1 = lax.rsqrt(jnp.sum(squares, axis=1, keepdims=True) / model_width + norm_eps)

    def third(step, pre):
        at = cut(step)
        low = (h1[:, at].astype(jnp.float32) * inv1).astype(jnp.bfloat16)
        normed1[:, at] = low
        return pre + dot_nt(low, w_ref[0, :, at])

    pre1 = lax.fori_loop(0, steps, third, zeros) * in_scale
    sig1 = jax.nn.sigmoid(pre1)
    act1 = jnp.where(layer_of == 1, pre1 * sig1, 0.0)
    slope1 = sig1 * (1.0 + pre1 * (1.0 - sig1))
    gp1 = jnp.where(layer_of == 1, grad_act1 * out_scale * slope1, 0.0)
    gp1_low = gp1.astype(jnp.bfloat16)
    inner = jnp.sum(gp1_low.astype(jnp.float32) * pre1, axis=1, keepdims=True)
    coef = inv1 * inv1 * inner / model_width
    factor = inv1 * in_scale

    def fourth(step, grad):
        at = cut(step)
        value = (
            g2[:, at].astype(jnp.float32)
            + factor * dot_nn(gp1_low, w_ref[0, :, at])
            - coef * h1[:, at].astype(jnp.float32)
        )
        low = value.astype(jnp.bfloat16)
        g1[:, at] = low
        return grad + dot_nt(low, w_ref[1, :, at])

    grad_act0 = lax.fori_loop(0, steps, fourth, zeros)
    slope0 = sig0 * (1.0 + pre0 * (1.0 - sig0))
    gp0 = jnp.where(layer_of == 0, grad_act0 * out_scale * slope0, 0.0)
    act_t = jnp.concatenate([act0.T, act1.T], axis=1).astype(jnp.bfloat16)
    gp_t = jnp.concatenate([gp0.T, gp1.T], axis=1).astype(jnp.bfloat16)

    def fifth(step, carry):
        at = cut(step)
        grad_out = dot_nn(act_t, jnp.concatenate([g1[:, at], g2[:, at]])) * out_scale
        grad_in = dot_nn(gp_t, jnp.concatenate([normed0[:, at], normed1[:, at]])) * in_scale
        for side in range(2):
            term = jnp.where(upper == side, grad_in, grad_out)
            for j in range(half):
                k = side * half + j
                out, place = places[k]
                outs[out][place, :, at] = term[j * ROWS : (j + 1) * ROWS].astype(jnp.bfloat16)
        return carry

    lax.fori_loop(0, steps, fifth, 0)


def adapter_grads(upper, normed, tokens, upstream, pieces, units, sets):
    model_width = tokens.shape[1]
    n_pieces = len(pieces)
    width = 1792 if model_width % 1792 == 0 else 128
    stacked = n_pieces * ROWS // 2
    places = {k: (out, place) for out, ks in enumerate(sets) for place, k in enumerate(ks)}
    whole = pl.BlockSpec(memory_space=pltpu.VMEM)
    return pl.pallas_call(
        functools.partial(adapter_kernel, n_pieces, places, units, width),
        out_shape=[jax.ShapeDtypeStruct((len(ks), ROWS, model_width), jnp.bfloat16) for ks in sets],
        in_specs=[pl.BlockSpec(memory_space=pltpu.SMEM)] + [whole] * (3 + n_pieces),
        out_specs=[whole] * len(sets),
        scratch_shapes=[
            pltpu.VMEM((2, stacked, model_width), jnp.bfloat16),
            pltpu.VMEM(tokens.shape, jnp.bfloat16),
            pltpu.VMEM(tokens.shape, jnp.bfloat16),
            pltpu.VMEM(tokens.shape, jnp.bfloat16),
        ],
        compiler_params=pltpu.CompilerParams(vmem_limit_bytes=16 * 2**20),
    )(upper, normed, tokens, upstream, *pieces)


def shards(inputs, cotangent, weights, first_moment, second_moment, anchor, momentum, fragment):
    tokens = inputs[0]
    upstream = cotangent[0]
    params = weights[0]
    layers, rows = params.shape[0], params.shape[1]
    model_width = tokens.shape[1]
    groups = lax.axis_size("fsdp")
    units = rows * 128 // model_width
    upper = (lax.axis_index("fsdp") >= groups // 2).astype(jnp.int32).reshape(1)
    compact = params.astype(jnp.bfloat16).reshape(layers * units, model_width)
    inputs_f32 = tokens.astype(jnp.float32)
    inv_rms = lax.rsqrt(jnp.mean(inputs_f32 * inputs_f32, axis=-1, keepdims=True) + norm_eps)
    pieces, inv_rms = gather_blocks(compact, "fsdp", inv_rms)
    normed = (inputs_f32 * inv_rms).astype(jnp.bfloat16)
    per_piece = ROWS // (layers * units)
    if per_piece > 1:
        pieces = [jnp.concatenate(pieces[i : i + per_piece]) for i in range(0, groups, per_piece)]

    count = fragment[0]
    chosen = jnp.remainder(count, layers)
    replicas = lax.axis_size("rep")
    total = anchor - lax.dynamic_index_in_dim(params, chosen, 0, keepdims=False)
    step = 1
    while step < replicas:
        total = total + swap(total, "rep", step)
        step *= 2
    upper, total = lax.optimization_barrier((upper, total))

    sets = output_sets(groups)
    if per_piece == 1:
        outs = adapter_grads(upper, normed, tokens, upstream, pieces, units, sets)
    else:
        (both,) = adapter_grads(upper, normed, tokens, upstream, pieces, units, [list(range(len(pieces)))])
        both = both.reshape(groups, layers * units, model_width)
        outs = [jnp.stack([both[k] for k in ks]) for ks in sets]
    even = {k: outs[-1][place] for place, k in enumerate(sets[-1])}
    summed = reduce_blocks(even, list(zip(sets, outs))[:-1], "fsdp").reshape(layers, rows, 128)
    gradient = summed / (tokens.shape[0] * groups)
    count_real = count.astype(jnp.float32)
    correct_one = 1.0 - jnp.exp(count_real * math.log(beta_one))
    correct_two = 1.0 - jnp.exp(count_real * math.log(beta_two))
    moment_one = beta_one * first_moment[0] + (1.0 - beta_one) * gradient
    moment_two = beta_two * second_moment[0] + (1.0 - beta_two) * gradient * gradient
    updated = params - inner_rate * (
        moment_one / correct_one / (jnp.sqrt(moment_two / correct_two) + adam_eps)
        + decay_rate * params
    )
    mean_delta = total / replicas
    new_velocity = outer_beta * momentum + mean_delta
    new_global = anchor - outer_rate * (mean_delta + outer_beta * new_velocity)
    selector = (jnp.arange(layers, dtype=jnp.int32) == chosen)[:, None, None]
    merged = jnp.where(selector, mixing * updated + (1.0 - mixing) * new_global[None], updated)
    return (merged[None], new_global, new_velocity)


def solution(mesh):
    placed = (
        P("rep", "fsdp", None),
        P("rep", "fsdp", None),
        P("rep", None, "fsdp", None),
        P("rep", None, "fsdp", None),
        P("rep", None, "fsdp", None),
        P("fsdp", None),
        P("fsdp", None),
        P(),
    )
    return jax.shard_map(
        shards,
        mesh=mesh,
        in_specs=placed,
        out_specs=(P("rep", None, "fsdp", None), P("fsdp", None), P("fsdp", None)),
        check_vma=False,
    )
```

```python
import functools
import math

import jax
import jax.numpy as jnp
from jax import lax
from jax.experimental import pallas as pl
from jax.experimental.pallas import tpu as pltpu
from jax.sharding import PartitionSpec as P

norm_eps = 1e-05
beta_one = 0.9
beta_two = 0.95
adam_eps = 1e-08
decay_rate = 0.1
inner_rate = 0.05
outer_rate = 0.7
outer_beta = 0.9
mixing = 0.5
ROWS = 8


def swap(value, axis, mask):
    size = lax.axis_size(axis)
    return lax.ppermute(value, axis, [(i, i ^ mask) for i in range(size)])


def after(value, *others):
    return lax.optimization_barrier((value, *others))[0]


def gather_blocks(own, axis, stage):
    size = lax.axis_size(axis)
    single = [k for k in range(4, size, 4) if k & (k - 1) == 0]
    others = [k for k in range(4, size, 4) if k & (k - 1)]
    own = own[None]
    have = {0: own}
    have[4] = swap(own, axis, 4)
    near = swap(own, axis, 2)
    for k in single[1:]:
        have[k] = swap(own, axis, k)
    done = stage((near, have[4]))
    for k in single[1:]:
        have[k] = after(have[k], done)
    for k in others:
        have[k] = swap(have[k & (k - 1)], axis, k & -k)
    first = jnp.concatenate([have[k] for k in single])
    second = jnp.concatenate([have[k] for k in others])
    far_first = swap(first, axis, 2)
    far_second = swap(second, axis, 2)
    sets = [
        ([0, 2] + single, jnp.concatenate([own, near, first])),
        (others + [k + 2 for k in single], jnp.concatenate([second, far_first])),
        ([k + 2 for k in others], far_second),
    ]
    crossed = [([k + 1 for k in ks], swap(blocks, axis, 1)) for ks, blocks in sets]
    return sets + crossed


def add_f32(left, right):
    return left.astype(jnp.float32) + right.astype(jnp.float32)


def reduce_blocks(blocks, odd_sets, axis):
    size = lax.axis_size(axis)
    left = dict(blocks)
    begun = None
    for ks, terms in odd_sets:
        came = swap(terms, axis, 1)
        if begun is not None:
            came = after(came, begun)
        for place, k in enumerate(ks):
            left[k - 1] = add_f32(left[k - 1], came[place])
        if begun is None:
            begun = left[ks[0] - 1] = left[ks[0] - 1].astype(jnp.bfloat16)

    def give(k, *earlier):
        part = after(left.pop(k).astype(jnp.bfloat16), *earlier)
        came = swap(part, axis, k & -k)
        left[k & (k - 1)] = left[k & (k - 1)] + came.astype(jnp.float32)
        return part

    earlier = ()
    for k in range(size - 4, -1, -4):
        give(k + 2, *earlier)
        if k:
            earlier = (give(k),)
    return left[0]


def output_sets(size):
    odd = list(range(size - 1, 0, -2))
    sends = [k for k in odd if k & 2]
    return [sends[:1], sends[1:], [k for k in odd if not k & 2], list(range(0, size, 2))]


def dot_nt(left, right):
    return lax.dot_general(left, right, (((1,), (1,)), ((), ())), preferred_element_type=jnp.float32)


def dot_nn(left, right, precision=None):
    return jnp.dot(left, right, preferred_element_type=jnp.float32, precision=precision)


def squares_of(value, total):
    value = value * value
    for j in range(0, value.shape[1], 128):
        total = total + value[:, j : j + 128]
    return total


def stage_kernel(h_ref, *refs):
    squares = refs[-1]
    width = 1024 if h_ref.shape[1] % 1024 == 0 else 128

    def step(at, total):
        cut = pl.ds(pl.multiple_of(at * width, width), width)
        return squares_of(h_ref[:, cut].astype(jnp.float32), total)

    squares[...] = lax.fori_loop(0, h_ref.shape[1] // width, step, jnp.zeros(squares.shape, jnp.float32))


def stage_tokens(tokens, early):
    return pl.pallas_call(
        stage_kernel,
        out_shape=jax.ShapeDtypeStruct((tokens.shape[0], 128), jnp.float32),
        in_specs=[pl.BlockSpec(memory_space=pltpu.VMEM)] + [pl.BlockSpec(memory_space=pl.ANY)] * len(early),
        out_specs=pl.BlockSpec(memory_space=pltpu.VMEM),
        compiler_params=pltpu.CompilerParams(vmem_limit_bytes=4 * 2**20),
    )(tokens, *early)


def adapter_kernel(n_arrays, sources, places, units, width, *refs):
    upper_ref, h0, g2, squares0 = refs[:4]
    arrays = refs[4 : 4 + n_arrays]
    outs = refs[4 + n_arrays : -2]
    n_pieces = len(sources)
    w_ref, h1 = refs[-2:]
    tokens, model_width = h0.shape
    stacked = n_pieces * ROWS // 2
    hidden = stacked // 2
    in_scale = model_width ** (-0.5)
    out_scale = hidden ** (-0.5)
    steps = model_width // width
    upper = upper_ref[0]
    half = n_pieces // 2
    w_in, w_out = pl.ds(0, stacked), pl.ds(stacked, stacked)
    layer_of = (lax.broadcasted_iota(jnp.int32, (tokens, stacked), 1) % (2 * units)) // units
    zeros = jnp.zeros((tokens, stacked), jnp.float32)
    no_squares = jnp.zeros((tokens, 128), jnp.float32)

    def cut(step):
        return pl.ds(pl.multiple_of(step * width, width), width)

    def inv_rms(squares):
        return lax.rsqrt(jnp.sum(squares, axis=1, keepdims=True) / model_width + norm_eps)

    def first(step, carry):
        pre, grad, cross = carry
        at = cut(step)
        for side in range(2):
            parts = []
            for k in range(side * half, side * half + half):
                array, place = sources[k]
                parts.append(arrays[array][place, :, at].astype(jnp.float32))
            rows = pl.ds(pl.multiple_of((side ^ upper) * stacked, stacked), stacked)
            w_ref[rows, at] = jnp.concatenate(parts).astype(jnp.bfloat16)
        pre = pre + dot_nt(h0[:, at], w_ref[w_in, at])
        grad = grad + dot_nt(g2[:, at], w_ref[w_out, at])
        cross = cross + dot_nt(w_ref[w_in, at], w_ref[w_out, at])
        return pre, grad, cross

    cross = jnp.zeros((stacked, stacked), jnp.float32)
    pre0, grad_act, cross = lax.fori_loop(0, steps, first, (zeros, zeros, cross))
    inv0 = inv_rms(squares0[...])
    pre0 = pre0 * (inv0 * in_scale)
    sig0 = jax.nn.sigmoid(pre0)
    act0 = jnp.where(layer_of == 0, pre0 * sig0, 0.0)
    act0_low = act0.astype(jnp.bfloat16)

    def second(step, carry):
        both, squares = carry
        at = cut(step)
        out = h0[:, at].astype(jnp.float32) + dot_nn(act0_low, w_ref[w_out, at]) * out_scale
        low = out.astype(jnp.bfloat16)
        h1[:, at] = low
        return both + dot_nt(low, w_ref[:, at]), squares_of(low.astype(jnp.float32), squares)

    both = jnp.zeros((tokens, 2 * stacked), jnp.float32)
    both, squares = lax.fori_loop(0, steps, second, (both, no_squares))
    inv1 = inv_rms(squares)
    pre1 = both[:, :stacked] * (inv1 * in_scale)
    sig1 = jax.nn.sigmoid(pre1)
    act1 = jnp.where(layer_of == 1, pre1 * sig1, 0.0)
    slope1 = sig1 * (1.0 + pre1 * (1.0 - sig1))
    gp1 = jnp.where(layer_of == 1, grad_act * out_scale * slope1, 0.0)
    gp1_low = gp1.astype(jnp.bfloat16)
    gp1 = gp1_low.astype(jnp.float32)
    coef = inv1 * inv1 * jnp.sum(gp1 * pre1, axis=1, keepdims=True) / model_width
    factor = inv1 * in_scale
    grad_act0 = (
        grad_act + factor * dot_nn(gp1, cross, lax.Precision.HIGHEST) - coef * both[:, stacked:]
    )
    slope0 = sig0 * (1.0 + pre0 * (1.0 - sig0))
    gp0 = jnp.where(layer_of == 0, grad_act0 * out_scale * slope0, 0.0)
    act_t = jnp.concatenate([act0.T, act1.T], axis=1).astype(jnp.bfloat16)
    gp_t = jnp.concatenate([(gp0 * inv0).T, (gp1 * inv1).T], axis=1).astype(jnp.bfloat16)

    def third(step, carry):
        at = cut(step)
        g1 = (
            g2[:, at].astype(jnp.float32)
            + factor * dot_nn(gp1_low, w_ref[w_in, at])
            - coef * h1[:, at].astype(jnp.float32)
        ).astype(jnp.bfloat16)
        grad_out = dot_nn(act_t, jnp.concatenate([g1, g2[:, at]]))
        grad_in = dot_nn(gp_t, jnp.concatenate([h0[:, at], h1[:, at]]))
        for side in range(2):
            term = jnp.where(upper == side, grad_in, grad_out)
            for j in range(half):
                out, place = places[side * half + j]
                outs[out][place, :, at] = term[j * ROWS : (j + 1) * ROWS].astype(jnp.bfloat16)
        return carry

    lax.fori_loop(0, steps, third, 0)


def places_of(sets):
    return {k: (at, place) for at, ks in enumerate(sets) for place, k in enumerate(ks)}


def adapter_grads(upper, tokens, upstream, squares, gathered, units, sets):
    model_width = tokens.shape[1]
    arrays = [array for _, array in gathered]
    sources = places_of([ks for ks, _ in gathered])
    places = places_of(sets)
    width = 1792 if model_width % 1792 == 0 else 128
    stacked = len(sources) * ROWS // 2
    whole = pl.BlockSpec(memory_space=pltpu.VMEM)
    return pl.pallas_call(
        functools.partial(adapter_kernel, len(arrays), sources, places, units, width),
        out_shape=[jax.ShapeDtypeStruct((len(ks), ROWS, model_width), jnp.bfloat16) for ks in sets],
        in_specs=[pl.BlockSpec(memory_space=pltpu.SMEM)] + [whole] * (3 + len(arrays)),
        out_specs=[whole] * len(sets),
        scratch_shapes=[
            pltpu.VMEM((2 * stacked, model_width), jnp.bfloat16),
            pltpu.VMEM(tokens.shape, jnp.bfloat16),
        ],
        compiler_params=pltpu.CompilerParams(vmem_limit_bytes=10 * 2**20),
    )(upper, tokens, upstream, squares, *arrays)


def shards(inputs, cotangent, weights, first_moment, second_moment, anchor, momentum, fragment):
    tokens = inputs[0]
    upstream = cotangent[0]
    params = weights[0]
    layers, rows = params.shape[0], params.shape[1]
    model_width = tokens.shape[1]
    groups = lax.axis_size("fsdp")
    units = rows * 128 // model_width
    hidden = units * groups // 2
    upper = (lax.axis_index("fsdp") >= groups // 2).astype(jnp.int32).reshape(1)
    compact = params.astype(jnp.bfloat16).reshape(layers * units, model_width)
    other = swap(params, "rep", 1)
    kept = []

    def stage(blocks):
        kept.append(stage_tokens(tokens, (*blocks, other)))
        return kept[0]

    gathered = gather_blocks(compact, "fsdp", stage)
    squares = kept[0]
    per_piece = ROWS // (layers * units)
    sets = output_sets(groups)
    if per_piece == 1:
        outs = adapter_grads(upper, tokens, upstream, squares, gathered, units, sets)
    else:
        blocks = {k: array[place] for ks, array in gathered for place, k in enumerate(ks)}
        blocks = jnp.stack([blocks[k] for k in range(groups)]).reshape(-1, ROWS, model_width)
        every = list(range(blocks.shape[0]))
        (both,) = adapter_grads(upper, tokens, upstream, squares, [(every, blocks)], units, [every])
        both = both.reshape(groups, layers * units, model_width)
        outs = [jnp.stack([both[k] for k in ks]) for ks in sets]
    even = {k: outs[-1][place] for place, k in enumerate(sets[-1])}
    summed = reduce_blocks(even, list(zip(sets, outs))[:-1], "fsdp").reshape(layers, rows, 128)
    scale = jnp.where(upper[0] == 1, hidden ** (-0.5), model_width ** (-0.5))
    gradient = summed * (scale / (tokens.shape[0] * groups))
    count = fragment[0]
    chosen = jnp.remainder(count, layers)

    def delta(values):
        return anchor - lax.dynamic_index_in_dim(values, chosen, 0, keepdims=False)

    replicas = lax.axis_size("rep")
    total = delta(params) + delta(other)
    step = 2
    while step < replicas:
        total = total + swap(total, "rep", step)
        step *= 2
    count_real = count.astype(jnp.float32)
    correct_one = 1.0 - jnp.exp(count_real * math.log(beta_one))
    correct_two = 1.0 - jnp.exp(count_real * math.log(beta_two))
    moment_one = beta_one * first_moment[0] + (1.0 - beta_one) * gradient
    moment_two = beta_two * second_moment[0] + (1.0 - beta_two) * gradient * gradient
    updated = params - inner_rate * (
        moment_one / correct_one / (jnp.sqrt(moment_two / correct_two) + adam_eps)
        + decay_rate * params
    )
    mean_delta = total / replicas
    new_velocity = outer_beta * momentum + mean_delta
    new_global = anchor - outer_rate * (mean_delta + outer_beta * new_velocity)
    selector = (jnp.arange(layers, dtype=jnp.int32) == chosen)[:, None, None]
    merged = jnp.where(selector, mixing * updated + (1.0 - mixing) * new_global[None], updated)
    return (merged[None], new_global, new_velocity)


def solution(mesh):
    placed = (
        P("rep", "fsdp", None),
        P("rep", "fsdp", None),
        P("rep", None, "fsdp", None),
        P("rep", None, "fsdp", None),
        P("rep", None, "fsdp", None),
        P("fsdp", None),
        P("fsdp", None),
        P(),
    )
    return jax.shard_map(
        shards,
        mesh=mesh,
        in_specs=placed,
        out_specs=(P("rep", None, "fsdp", None), P("fsdp", None), P("fsdp", None)),
        check_vma=False,
    )
```

```python
import functools
import math

import jax
import jax.numpy as jnp
from jax import lax
from jax.experimental import pallas as pl
from jax.experimental.pallas import tpu as pltpu
from jax.sharding import PartitionSpec as P

norm_eps = 1e-05
beta_one = 0.9
beta_two = 0.95
adam_eps = 1e-08
decay_rate = 0.1
inner_rate = 0.05
outer_rate = 0.7
outer_beta = 0.9
mixing = 0.5
ROWS = 8


def swap(value, axis, mask):
    size = lax.axis_size(axis)
    return lax.ppermute(value, axis, [(i, i ^ mask) for i in range(size)])


def after(value, *others):
    return lax.optimization_barrier((value, *others))[0]


def gather_blocks(own, axis, stage, late):
    size = lax.axis_size(axis)
    single = [k for k in range(4, size, 4) if k & (k - 1) == 0]
    others = [k for k in range(4, size, 4) if k & (k - 1)]
    own = own[None]
    have = {0: own}
    have[4] = swap(own, axis, 4)
    near = swap(own, axis, 2)
    for k in single[1:]:
        have[k] = swap(own, axis, k)
    done = stage((near, have[4]))
    for k in single[1:]:
        have[k] = after(have[k], done)
    for k in others:
        have[k] = swap(have[k & (k - 1)], axis, k & -k)
    first = jnp.concatenate([have[k] for k in single])
    second = jnp.concatenate([have[k] for k in others])
    far_first = swap(first, axis, 2)
    far_second = swap(second, axis, 2)
    sets = [
        ([0, 2] + single, after(jnp.concatenate([own, near, first]), late)),
        (others + [k + 2 for k in single], jnp.concatenate([second, far_first])),
        ([k + 2 for k in others], far_second),
    ]
    crossed = [([k + 1 for k in ks], swap(blocks, axis, 1)) for ks, blocks in sets]
    return sets + crossed


def add_f32(left, right):
    return left.astype(jnp.float32) + right.astype(jnp.float32)


def output_sets(size):
    tops = list(range(size - 4, -1, -4))
    half = len(tops) // 2
    parts = [[k + 2 for k in tops[:half]], [k + 2 for k in tops[half:]], tops]
    return [[k + 1 for k in ks] for ks in parts] + parts


def reduce_blocks(outs, axis):
    size = lax.axis_size(axis)
    tops = list(range(size - 4, -1, -4))
    half = len(tops) // 2
    came = [swap(odd, axis, 1) for odd in outs[:3]]
    sums = add_f32(outs[3], came[0]).astype(jnp.bfloat16)
    near = swap(sums, axis, 2)
    came[1] = after(came[1], sums)
    sums = add_f32(outs[4], came[1]).astype(jnp.bfloat16)
    rest = swap(after(sums, near), axis, 2)
    came[2] = after(came[2], sums)
    kept = add_f32(outs[5], came[2])
    left = {}
    for at, k in enumerate(tops):
        if at == half:
            rest = after(rest, part)
        arrived = near[at] if at < half else rest[at - half]
        left[k] = left.get(k, 0.0) + kept[at] + arrived.astype(jnp.float32)
        if k:
            part = left[k].astype(jnp.bfloat16)
            moved = swap(part, axis, k & -k).astype(jnp.float32)
            left[k & (k - 1)] = left.get(k & (k - 1), 0.0) + moved
    return left[0]


def dot(left, right, precision=None):
    return jnp.dot(left, right, preferred_element_type=jnp.float32, precision=precision)


def squares_of(value, total):
    value = value * value
    for j in range(0, value.shape[1], 128):
        total = total + value[:, j : j + 128]
    return total


def stage_kernel(h_ref, *refs):
    squares = refs[-1]
    width = 1024 if h_ref.shape[1] % 1024 == 0 else 128

    def step(at, total):
        cut = pl.ds(pl.multiple_of(at * width, width), width)
        return squares_of(h_ref[:, cut].astype(jnp.float32), total)

    squares[...] = lax.fori_loop(0, h_ref.shape[1] // width, step, jnp.zeros(squares.shape, jnp.float32))


def stage_tokens(tokens, early):
    return pl.pallas_call(
        stage_kernel,
        out_shape=jax.ShapeDtypeStruct((tokens.shape[0], 128), jnp.float32),
        in_specs=[pl.BlockSpec(memory_space=pltpu.VMEM)] + [pl.BlockSpec(memory_space=pl.ANY)] * len(early),
        out_specs=pl.BlockSpec(memory_space=pltpu.VMEM),
        compiler_params=pltpu.CompilerParams(vmem_limit_bytes=4 * 2**20),
    )(tokens, *early)


def adapter_kernel(n_arrays, sources, places, units, width, *refs):
    upper_ref, h0, g2, squares0 = refs[:4]
    arrays = refs[4 : 4 + n_arrays]
    outs = refs[4 + n_arrays : -3]
    w_ref, wt_ref, h1 = refs[-3:]
    n_pieces = len(sources)
    tokens, model_width = h0.shape
    stacked = n_pieces * ROWS // 2
    hidden = stacked // 2
    in_scale = model_width ** (-0.5)
    out_scale = hidden ** (-0.5)
    steps = model_width // 2 // width
    upper = upper_ref[0]
    half = n_pieces // 2
    w_in, w_out = pl.ds(0, stacked), pl.ds(stacked, stacked)
    layer_of = (lax.broadcasted_iota(jnp.int32, (tokens, stacked), 1) % (2 * units)) // units
    no_squares = jnp.zeros((tokens, 128), jnp.float32)

    def cut(step, side=0):
        return pl.ds(pl.multiple_of(side * (model_width // 2) + step * width, width), width)

    def inv_rms(squares):
        return lax.rsqrt(jnp.sum(squares, axis=1, keepdims=True) / model_width + norm_eps)

    def first(step, total):
        low = cut(step)
        for part in range(2):
            values = []
            for k in range(part * half, part * half + half):
                array, place = sources[k]
                values.append(arrays[array][place, :, low].astype(jnp.float32))
            rows = pl.ds(pl.multiple_of((part ^ upper) * stacked, stacked), stacked)
            for side in range(2):
                block = jnp.concatenate([v[side * ROWS : (side + 1) * ROWS] for v in values])
                w_ref[rows, cut(step, side)] = block.astype(jnp.bfloat16)
        for side in range(2):
            at = cut(step, side)
            turned = w_ref[:, at].T
            wt_ref[at, :] = turned
            total = total + dot(jnp.concatenate([h0[:, at], g2[:, at], w_ref[w_in, at]]), turned)
        return total

    total = jnp.zeros((2 * tokens + stacked, 2 * stacked), jnp.float32)
    total = lax.fori_loop(0, steps, first, total)
    pre0 = total[:tokens, :stacked]
    grad_act = total[tokens : 2 * tokens, stacked:]
    cross = total[2 * tokens :, stacked:]
    inv0 = inv_rms(squares0[...])
    pre0 = pre0 * (inv0 * in_scale)
    sig0 = jax.nn.sigmoid(pre0)
    act0 = jnp.where(layer_of == 0, pre0 * sig0, 0.0)
    act0_low = act0.astype(jnp.bfloat16)

    def second(step, carry):
        both, squares = carry
        for side in range(2):
            at = cut(step, side)
            out = h0[:, at].astype(jnp.float32) + dot(act0_low, w_ref[w_out, at]) * out_scale
            low = out.astype(jnp.bfloat16)
            h1[:, at] = low
            both = both + dot(low, wt_ref[at, :])
            squares = squares_of(low.astype(jnp.float32), squares)
        return both, squares

    both = jnp.zeros((tokens, 2 * stacked), jnp.float32)
    both, squares = lax.fori_loop(0, steps, second, (both, no_squares))
    inv1 = inv_rms(squares)
    pre1 = both[:, :stacked] * (inv1 * in_scale)
    sig1 = jax.nn.sigmoid(pre1)
    act1 = jnp.where(layer_of == 1, pre1 * sig1, 0.0)
    slope1 = sig1 * (1.0 + pre1 * (1.0 - sig1))
    gp1 = jnp.where(layer_of == 1, grad_act * out_scale * slope1, 0.0)
    gp1_low = gp1.astype(jnp.bfloat16)
    gp1 = gp1_low.astype(jnp.float32)
    coef = inv1 * inv1 * jnp.sum(gp1 * pre1, axis=1, keepdims=True) / model_width
    factor = inv1 * in_scale
    grad_act0 = grad_act + factor * dot(gp1, cross, lax.Precision.HIGHEST) - coef * both[:, stacked:]
    slope0 = sig0 * (1.0 + pre0 * (1.0 - sig0))
    gp0 = jnp.where(layer_of == 0, grad_act0 * out_scale * slope0, 0.0)
    act_t = jnp.concatenate([act0.T, act1.T], axis=1).astype(jnp.bfloat16)
    gp_t = jnp.concatenate([(gp0 * inv0).T, (gp1 * inv1).T], axis=1).astype(jnp.bfloat16)

    def third(step, carry):
        terms = []
        for side in range(2):
            at = cut(step, side)
            g1 = (
                g2[:, at].astype(jnp.float32)
                + factor * dot(gp1_low, w_ref[w_in, at])
                - coef * h1[:, at].astype(jnp.float32)
            ).astype(jnp.bfloat16)
            grad_out = dot(act_t, jnp.concatenate([g1, g2[:, at]]))
            grad_in = dot(gp_t, jnp.concatenate([h0[:, at], h1[:, at]]))
            terms.append([jnp.where(upper == part, grad_in, grad_out) for part in range(2)])
        for k in range(n_pieces):
            out, place = places[k]
            part, j = k // half, k % half
            rows = [terms[side][part][j * ROWS : (j + 1) * ROWS] for side in range(2)]
            outs[out][place, :, cut(step)] = jnp.concatenate(rows).astype(jnp.bfloat16)
        return carry

    lax.fori_loop(0, steps, third, 0)


def places_of(sets):
    return {k: (at, place) for at, ks in enumerate(sets) for place, k in enumerate(ks)}


def adapter_grads(upper, tokens, upstream, squares, gathered, units, sets):
    model_width = tokens.shape[1]
    arrays = [array for _, array in gathered]
    sources = places_of([ks for ks, _ in gathered])
    places = places_of(sets)
    width = 512 if model_width % 1024 == 0 else 128
    stacked = len(sources) * ROWS // 2
    whole = pl.BlockSpec(memory_space=pltpu.VMEM)
    shapes = [(len(ks), 2 * ROWS, model_width // 2) for ks in sets]
    return pl.pallas_call(
        functools.partial(adapter_kernel, len(arrays), sources, places, units, width),
        out_shape=[jax.ShapeDtypeStruct(shape, jnp.bfloat16) for shape in shapes],
        in_specs=[pl.BlockSpec(memory_space=pltpu.SMEM)] + [whole] * (3 + len(arrays)),
        out_specs=[whole] * len(sets),
        scratch_shapes=[
            pltpu.VMEM((2 * stacked, model_width), jnp.bfloat16),
            pltpu.VMEM((model_width, 2 * stacked), jnp.bfloat16),
            pltpu.VMEM(tokens.shape, jnp.bfloat16),
        ],
        compiler_params=pltpu.CompilerParams(vmem_limit_bytes=12 * 2**20),
    )(upper, tokens, upstream, squares, *arrays)


def shards(inputs, cotangent, weights, first_moment, second_moment, anchor, momentum, fragment):
    tokens = inputs[0]
    upstream = cotangent[0]
    params = weights[0]
    layers, rows = params.shape[0], params.shape[1]
    model_width = tokens.shape[1]
    groups = lax.axis_size("fsdp")
    replicas = lax.axis_size("rep")
    units = rows * 128 // model_width
    hidden = units * groups // 2
    piece = layers * units
    upper = (lax.axis_index("fsdp") >= groups // 2).astype(jnp.int32).reshape(1)
    count = fragment[0]
    chosen = jnp.remainder(count, layers)
    count_real = count.astype(jnp.float32)
    correct_one = 1.0 - jnp.exp(count_real * math.log(beta_one))
    correct_two = 1.0 - jnp.exp(count_real * math.log(beta_two))
    scale = jnp.where(upper[0] == 1, hidden ** (-0.5), model_width ** (-0.5))
    scale = scale / (tokens.shape[0] * groups)
    compact = params.astype(jnp.bfloat16).reshape(piece, 2, model_width // 2)
    compact = compact.transpose(1, 0, 2).reshape(2 * piece, model_width // 2)
    compact, upper, chosen, correct_one, correct_two, scale = lax.optimization_barrier(
        (compact, upper, chosen, correct_one, correct_two, scale)
    )
    other = swap(params, "rep", 1)
    kept = []

    def stage(blocks):
        kept.append(stage_tokens(tokens, blocks))
        return kept[0]

    gathered = gather_blocks(compact, "fsdp", stage, other)
    squares = kept[0]

    sets = output_sets(groups)
    if piece == ROWS:
        outs = adapter_grads(upper, tokens, upstream, squares, gathered, units, sets)
    else:
        merged = ROWS // piece
        blocks = {k: array[place] for ks, array in gathered for place, k in enumerate(ks)}
        blocks = jnp.stack([blocks[k] for k in range(groups)])
        blocks = blocks.reshape(groups // merged, merged, 2, piece, model_width // 2)
        blocks = blocks.transpose(0, 2, 1, 3, 4).reshape(groups // merged, 2 * ROWS, model_width // 2)
        every = list(range(groups // merged))
        (both,) = adapter_grads(upper, tokens, upstream, squares, [(every, blocks)], units, [every])
        both = both.reshape(groups // merged, 2, merged, piece, model_width // 2)
        both = both.transpose(0, 2, 1, 3, 4).reshape(groups, 2 * piece, model_width // 2)
        outs = [jnp.stack([both[k] for k in ks]) for ks in sets]
    summed = reduce_blocks(outs, "fsdp").reshape(2, piece, model_width // 2)
    summed = summed.transpose(1, 0, 2).reshape(layers, rows, 128)
    gradient = summed * scale

    def delta(values):
        return anchor - lax.dynamic_index_in_dim(values, chosen, 0, keepdims=False)

    total = delta(params) + delta(other)
    step = 2
    while step < replicas:
        total = total + swap(total, "rep", step)
        step *= 2
    moment_one = beta_one * first_moment[0] + (1.0 - beta_one) * gradient
    moment_two = beta_two * second_moment[0] + (1.0 - beta_two) * gradient * gradient
    updated = params - inner_rate * (
        moment_one / correct_one / (jnp.sqrt(moment_two / correct_two) + adam_eps)
        + decay_rate * params
    )
    mean_delta = total / replicas
    new_velocity = outer_beta * momentum + mean_delta
    new_global = anchor - outer_rate * (mean_delta + outer_beta * new_velocity)
    selector = (jnp.arange(layers, dtype=jnp.int32) == chosen)[:, None, None]
    merged = jnp.where(selector, mixing * updated + (1.0 - mixing) * new_global[None], updated)
    return (merged[None], new_global, new_velocity)


def solution(mesh):
    placed = (
        P("rep", "fsdp", None),
        P("rep", "fsdp", None),
        P("rep", None, "fsdp", None),
        P("rep", None, "fsdp", None),
        P("rep", None, "fsdp", None),
        P("fsdp", None),
        P("fsdp", None),
        P(),
    )
    return jax.shard_map(
        shards,
        mesh=mesh,
        in_specs=placed,
        out_specs=(P("rep", None, "fsdp", None), P("fsdp", None), P("fsdp", None)),
        check_vma=False,
    )
```

```python
import functools
import math

import jax
import jax.numpy as jnp
from jax import lax
from jax.experimental import pallas as pl
from jax.experimental.pallas import tpu as pltpu
from jax.sharding import PartitionSpec as P

norm_eps = 1e-05
beta_one = 0.9
beta_two = 0.95
adam_eps = 1e-08
decay_rate = 0.1
inner_rate = 0.05
outer_rate = 0.7
outer_beta = 0.9
mixing = 0.5
ROWS = 8


def swap(value, axis, mask):
    size = lax.axis_size(axis)
    return lax.ppermute(value, axis, [(i, i ^ mask) for i in range(size)])


def after(value, *others):
    return lax.optimization_barrier((value, *others))[0]


def gather_blocks(own, axis, stage, late):
    size = lax.axis_size(axis)
    single = [k for k in range(4, size, 4) if k & (k - 1) == 0]
    others = [k for k in range(4, size, 4) if k & (k - 1)]
    own = own[None]
    have = {0: own}
    for k in reversed(single):
        have[k] = swap(own, axis, k)
    near = swap(own, axis, 2)
    for k in others:
        have[k] = swap(have[k & (k - 1)], axis, k & -k)
    first = jnp.concatenate([have[k] for k in single])
    second = jnp.concatenate([have[k] for k in others])
    far_first = swap(first, axis, 2)
    second = after(second, stage((have[single[-1]],)))
    far_second = swap(second, axis, 2)
    sets = [
        ([0, 2] + single, after(jnp.concatenate([own, near, first]), late)),
        (others + [k + 2 for k in single + others], jnp.concatenate([second, far_first, far_second])),
    ]
    crossed = [([k + 1 for k in ks], swap(blocks, axis, 1)) for ks, blocks in sets]
    return sets + crossed


def add_f32(left, right):
    return left.astype(jnp.float32) + right.astype(jnp.float32)


def output_sets(size):
    tops = list(range(size - 4, -1, -4))
    half = len(tops) // 2
    parts = [[k + 2 for k in tops[:half]], [k + 2 for k in tops[half:]], tops]
    return [[k + 1 for k in ks] for ks in parts] + parts


def reduce_blocks(outs, axis):
    size = lax.axis_size(axis)
    tops = list(range(size - 4, -1, -4))
    half = len(tops) // 2
    came = swap(outs[0], axis, 1)
    sums = add_f32(outs[3], came).astype(jnp.bfloat16)
    near = [swap(sums[at], axis, 2) for at in range(half)]
    odd, last_odd, sums = lax.optimization_barrier((outs[1], outs[2], sums))
    came = swap(odd, axis, 1)
    sums = add_f32(outs[4], came).astype(jnp.bfloat16)
    rest = swap(sums, axis, 2)
    near[0] = after(near[0], sums)
    kept = add_f32(outs[5], swap(last_odd, axis, 1))
    left = {}
    for at, k in enumerate(tops):
        if at == half:
            rest = after(rest, part)
        arrived = near[at] if at < half else rest[at - half]
        left[k] = left.get(k, 0.0) + kept[at] + arrived.astype(jnp.float32)
        if k:
            part = left[k].astype(jnp.bfloat16)
            moved = swap(part, axis, k & -k).astype(jnp.float32)
            left[k & (k - 1)] = left.get(k & (k - 1), 0.0) + moved
    return left[0]


def dot_nt(left, right):
    return lax.dot_general(left, right, (((1,), (1,)), ((), ())), preferred_element_type=jnp.float32)


def dot(left, right, precision=None):
    return jnp.dot(left, right, preferred_element_type=jnp.float32, precision=precision)


def squares_of(value, total):
    value = value * value
    for j in range(0, value.shape[1], 128):
        total = total + value[:, j : j + 128]
    return total


def stage_kernel(h_ref, *refs):
    squares = refs[-1]
    width = 1024 if h_ref.shape[1] % 1024 == 0 else 128

    def step(at, total):
        cut = pl.ds(pl.multiple_of(at * width, width), width)
        return squares_of(h_ref[:, cut].astype(jnp.float32), total)

    squares[...] = lax.fori_loop(0, h_ref.shape[1] // width, step, jnp.zeros(squares.shape, jnp.float32))


def stage_tokens(tokens, early):
    return pl.pallas_call(
        stage_kernel,
        out_shape=jax.ShapeDtypeStruct((tokens.shape[0], 128), jnp.float32),
        in_specs=[pl.BlockSpec(memory_space=pltpu.VMEM)] + [pl.BlockSpec(memory_space=pl.ANY)] * len(early),
        out_specs=pl.BlockSpec(memory_space=pltpu.VMEM),
        compiler_params=pltpu.CompilerParams(vmem_limit_bytes=4 * 2**20),
    )(tokens, *early)


def adapter_kernel(n_arrays, sources, places, units, width, *refs):
    upper_ref, h0, g2, squares0 = refs[:4]
    arrays = refs[4 : 4 + n_arrays]
    outs = refs[4 + n_arrays : -2]
    w_ref, h1 = refs[-2:]
    n_pieces = len(sources)
    tokens, model_width = h0.shape
    stacked = n_pieces * ROWS // 2
    hidden = stacked // 2
    in_scale = model_width ** (-0.5)
    out_scale = hidden ** (-0.5)
    steps = model_width // 2 // width
    upper = upper_ref[0]
    half = n_pieces // 2
    w_in, w_out = pl.ds(0, stacked), pl.ds(stacked, stacked)
    layer_of = (lax.broadcasted_iota(jnp.int32, (tokens, stacked), 1) % (2 * units)) // units
    no_squares = jnp.zeros((tokens, 128), jnp.float32)

    def cut(step, side=0):
        return pl.ds(pl.multiple_of(side * (model_width // 2) + step * width, width), width)

    def inv_rms(squares):
        return lax.rsqrt(jnp.sum(squares, axis=1, keepdims=True) / model_width + norm_eps)

    def first(step, total):
        low = cut(step)
        for part in range(2):
            values = []
            for k in range(part * half, part * half + half):
                array, place = sources[k]
                values.append(arrays[array][place, :, low].astype(jnp.float32))
            rows = pl.ds(pl.multiple_of((part ^ upper) * stacked, stacked), stacked)
            for side in range(2):
                block = jnp.concatenate([v[side * ROWS : (side + 1) * ROWS] for v in values])
                w_ref[rows, cut(step, side)] = block.astype(jnp.bfloat16)
        for side in range(2):
            at = cut(step, side)
            total = total + dot_nt(jnp.concatenate([h0[:, at], g2[:, at], w_ref[w_in, at]]), w_ref[:, at])
        return total

    total = jnp.zeros((2 * tokens + stacked, 2 * stacked), jnp.float32)
    total = lax.fori_loop(0, steps, first, total)
    pre0 = total[:tokens, :stacked]
    grad_act = total[tokens : 2 * tokens, stacked:]
    cross = total[2 * tokens :, stacked:]
    inv0 = inv_rms(squares0[...])
    pre0 = pre0 * (inv0 * in_scale)
    sig0 = jax.nn.sigmoid(pre0)
    act0 = jnp.where(layer_of == 0, pre0 * sig0, 0.0)
    act0_low = act0.astype(jnp.bfloat16)

    def second(step, carry):
        both, squares = carry
        for side in range(2):
            at = cut(step, side)
            out = h0[:, at].astype(jnp.float32) + dot(act0_low, w_ref[w_out, at]) * out_scale
            low = out.astype(jnp.bfloat16)
            h1[:, at] = low
            both = both + dot_nt(low, w_ref[:, at])
            squares = squares_of(low.astype(jnp.float32), squares)
        return both, squares

    both = jnp.zeros((tokens, 2 * stacked), jnp.float32)
    both, squares = lax.fori_loop(0, steps, second, (both, no_squares))
    inv1 = inv_rms(squares)
    pre1 = both[:, :stacked] * (inv1 * in_scale)
    sig1 = jax.nn.sigmoid(pre1)
    act1 = jnp.where(layer_of == 1, pre1 * sig1, 0.0)
    slope1 = sig1 * (1.0 + pre1 * (1.0 - sig1))
    gp1 = jnp.where(layer_of == 1, grad_act * out_scale * slope1, 0.0)
    gp1_low = gp1.astype(jnp.bfloat16)
    gp1 = gp1_low.astype(jnp.float32)
    coef = inv1 * inv1 * jnp.sum(gp1 * pre1, axis=1, keepdims=True) / model_width
    factor = inv1 * in_scale
    grad_act0 = grad_act + factor * dot(gp1, cross, lax.Precision.HIGHEST) - coef * both[:, stacked:]
    slope0 = sig0 * (1.0 + pre0 * (1.0 - sig0))
    gp0 = jnp.where(layer_of == 0, grad_act0 * out_scale * slope0, 0.0)
    act_t = jnp.concatenate([act0.T, act1.T], axis=1).astype(jnp.bfloat16)
    gp_t = jnp.concatenate([(gp0 * inv0).T, (gp1 * inv1).T], axis=1).astype(jnp.bfloat16)

    def third(step, carry):
        terms = []
        for side in range(2):
            at = cut(step, side)
            g1 = (
                g2[:, at].astype(jnp.float32)
                + factor * dot(gp1_low, w_ref[w_in, at])
                - coef * h1[:, at].astype(jnp.float32)
            ).astype(jnp.bfloat16)
            grad_out = dot(act_t, jnp.concatenate([g1, g2[:, at]]))
            grad_in = dot(gp_t, jnp.concatenate([h0[:, at], h1[:, at]]))
            terms.append([jnp.where(upper == part, grad_in, grad_out) for part in range(2)])
        for k in range(n_pieces):
            out, place = places[k]
            part, j = k // half, k % half
            rows = [terms[side][part][j * ROWS : (j + 1) * ROWS] for side in range(2)]
            outs[out][place, :, cut(step)] = jnp.concatenate(rows).astype(jnp.bfloat16)
        return carry

    lax.fori_loop(0, steps, third, 0)


def places_of(sets):
    return {k: (at, place) for at, ks in enumerate(sets) for place, k in enumerate(ks)}


def adapter_grads(upper, tokens, upstream, squares, gathered, units, sets):
    model_width = tokens.shape[1]
    arrays = [array for _, array in gathered]
    sources = places_of([ks for ks, _ in gathered])
    places = places_of(sets)
    width = 1792 if model_width % 3584 == 0 else 128
    stacked = len(sources) * ROWS // 2
    whole = pl.BlockSpec(memory_space=pltpu.VMEM)
    shapes = [(len(ks), 2 * ROWS, model_width // 2) for ks in sets]
    return pl.pallas_call(
        functools.partial(adapter_kernel, len(arrays), sources, places, units, width),
        out_shape=[jax.ShapeDtypeStruct(shape, jnp.bfloat16) for shape in shapes],
        in_specs=[pl.BlockSpec(memory_space=pltpu.SMEM)] + [whole] * (3 + len(arrays)),
        out_specs=[whole] * len(sets),
        scratch_shapes=[
            pltpu.VMEM((2 * stacked, model_width), jnp.bfloat16),
            pltpu.VMEM(tokens.shape, jnp.bfloat16),
        ],
        compiler_params=pltpu.CompilerParams(vmem_limit_bytes=14 * 2**20),
    )(upper, tokens, upstream, squares, *arrays)


def shards(inputs, cotangent, weights, first_moment, second_moment, anchor, momentum, fragment):
    tokens = inputs[0]
    upstream = cotangent[0]
    params = weights[0]
    layers, rows = params.shape[0], params.shape[1]
    model_width = tokens.shape[1]
    groups = lax.axis_size("fsdp")
    replicas = lax.axis_size("rep")
    units = rows * 128 // model_width
    hidden = units * groups // 2
    piece = layers * units
    upper = (lax.axis_index("fsdp") >= groups // 2).astype(jnp.int32).reshape(1)
    count = fragment[0]
    chosen = jnp.remainder(count, layers)
    count_real = count.astype(jnp.float32)
    correct_one = 1.0 - jnp.exp(count_real * math.log(beta_one))
    correct_two = 1.0 - jnp.exp(count_real * math.log(beta_two))
    scale = jnp.where(upper[0] == 1, hidden ** (-0.5), model_width ** (-0.5))
    scale = scale / (tokens.shape[0] * groups)
    compact = params.astype(jnp.bfloat16).reshape(piece, 2, model_width // 2)
    compact = compact.transpose(1, 0, 2).reshape(2 * piece, model_width // 2)
    compact, upper, chosen, correct_one, correct_two, scale = lax.optimization_barrier(
        (compact, upper, chosen, correct_one, correct_two, scale)
    )
    other = swap(params, "rep", 1)
    kept = []

    def stage(blocks):
        kept.append(stage_tokens(tokens, blocks))
        return kept[0]

    gathered = gather_blocks(compact, "fsdp", stage, other)
    squares = kept[0]

    sets = output_sets(groups)
    if piece == ROWS:
        outs = adapter_grads(upper, tokens, upstream, squares, gathered, units, sets)
    else:
        merged = ROWS // piece
        blocks = {k: array[place] for ks, array in gathered for place, k in enumerate(ks)}
        blocks = jnp.stack([blocks[k] for k in range(groups)])
        blocks = blocks.reshape(groups // merged, merged, 2, piece, model_width // 2)
        blocks = blocks.transpose(0, 2, 1, 3, 4).reshape(groups // merged, 2 * ROWS, model_width // 2)
        every = list(range(groups // merged))
        (both,) = adapter_grads(upper, tokens, upstream, squares, [(every, blocks)], units, [every])
        both = both.reshape(groups // merged, 2, merged, piece, model_width // 2)
        both = both.transpose(0, 2, 1, 3, 4).reshape(groups, 2 * piece, model_width // 2)
        outs = [jnp.stack([both[k] for k in ks]) for ks in sets]
    summed = reduce_blocks(outs, "fsdp").reshape(2, piece, model_width // 2)
    summed = summed.transpose(1, 0, 2).reshape(layers, rows, 128)
    gradient = summed * scale

    def delta(values):
        return anchor - lax.dynamic_index_in_dim(values, chosen, 0, keepdims=False)

    total = delta(params) + delta(other)
    step = 2
    while step < replicas:
        total = total + swap(total, "rep", step)
        step *= 2
    moment_one = beta_one * first_moment[0] + (1.0 - beta_one) * gradient
    moment_two = beta_two * second_moment[0] + (1.0 - beta_two) * gradient * gradient
    updated = params - inner_rate * (
        moment_one / correct_one / (jnp.sqrt(moment_two / correct_two) + adam_eps)
        + decay_rate * params
    )
    mean_delta = total / replicas
    new_velocity = outer_beta * momentum + mean_delta
    new_global = anchor - outer_rate * (mean_delta + outer_beta * new_velocity)
    selector = (jnp.arange(layers, dtype=jnp.int32) == chosen)[:, None, None]
    merged = jnp.where(selector, mixing * updated + (1.0 - mixing) * new_global[None], updated)
    return (merged[None], new_global, new_velocity)


def solution(mesh):
    placed = (
        P("rep", "fsdp", None),
        P("rep", "fsdp", None),
        P("rep", None, "fsdp", None),
        P("rep", None, "fsdp", None),
        P("rep", None, "fsdp", None),
        P("fsdp", None),
        P("fsdp", None),
        P(),
    )
    return jax.shard_map(
        shards,
        mesh=mesh,
        in_specs=placed,
        out_specs=(P("rep", None, "fsdp", None), P("fsdp", None), P("fsdp", None)),
        check_vma=False,
    )
```

```python
import functools
import math

import jax
import jax.numpy as jnp
from jax import lax
from jax.experimental import pallas as pl
from jax.experimental.pallas import tpu as pltpu
from jax.sharding import PartitionSpec as P

norm_eps = 1e-05
beta_one = 0.9
beta_two = 0.95
adam_eps = 1e-08
decay_rate = 0.1
inner_rate = 0.05
outer_rate = 0.7
outer_beta = 0.9
mixing = 0.5
ROWS = 8


def swap(value, axis, mask):
    size = lax.axis_size(axis)
    return lax.ppermute(value, axis, [(i, i ^ mask) for i in range(size)])


def after(value, *others):
    return lax.optimization_barrier((value, *others))[0]


def gather_blocks(own, axis, stage, late):
    size = lax.axis_size(axis)
    single = [k for k in range(4, size, 4) if k & (k - 1) == 0]
    others = [k for k in range(4, size, 4) if k & (k - 1)]
    own = own[None]
    have = {0: own}
    for k in reversed(single):
        have[k] = swap(own, axis, k)
    near = swap(own, axis, 2)
    for k in others:
        have[k] = swap(have[k & (k - 1)], axis, k & -k)
    first = jnp.concatenate([have[k] for k in single])
    second = jnp.concatenate([have[k] for k in others])
    far_first = swap(first, axis, 2)
    second = after(second, stage((have[single[-1]],)))
    far_second = swap(second, axis, 2)
    sets = [
        ([0, 2] + single, after(jnp.concatenate([own, near, first]), late)),
        (others + [k + 2 for k in single + others], jnp.concatenate([second, far_first, far_second])),
    ]
    crossed = [([k + 1 for k in ks], swap(blocks, axis, 1)) for ks, blocks in sets]
    return sets + crossed


def add_f32(left, right):
    return left.astype(jnp.float32) + right.astype(jnp.float32)


def output_sets(size):
    tops = list(range(size - 4, -1, -4))
    even = [k + 2 for k in tops] + tops
    return [[k + 1 for k in even], even]


def reduce_blocks(odd, even, axis):
    size = lax.axis_size(axis)
    tops = list(range(size - 4, -1, -4))
    half = len(tops) // 2
    came = swap(odd, axis, 1)
    sums = add_f32(even[: len(tops)], came[: len(tops)]).astype(jnp.bfloat16)
    near = [swap(sums[at], axis, 2) for at in range(half)]
    rest = swap(sums[half:], axis, 2)
    came = after(came, sums)
    kept = add_f32(even[len(tops) :], came[len(tops) :])
    parts = []
    left = {}
    for at, k in enumerate(tops):
        if at == half:
            rest = after(rest, part)
        arrived = near[at] if at < half else rest[at - half]
        if k:
            left[k] = left.get(k, 0.0) + kept[at] + arrived.astype(jnp.float32)
            part = left[k].astype(jnp.bfloat16)
            moved = swap(part, axis, k & -k)
            if k & (k - 1):
                left[k & (k - 1)] = left.get(k & (k - 1), 0.0) + moved.astype(jnp.float32)
            else:
                parts.append(moved)
    return [kept[-1], rest[-1]] + parts


def dot_nt(left, right):
    return lax.dot_general(left, right, (((1,), (1,)), ((), ())), preferred_element_type=jnp.float32)


def dot(left, right, precision=None):
    return jnp.dot(left, right, preferred_element_type=jnp.float32, precision=precision)


def squares_of(value, total):
    value = value * value
    for j in range(0, value.shape[1], 128):
        total = total + value[:, j : j + 128]
    return total


def stage_kernel(h_ref, *refs):
    squares = refs[-1]
    width = 1024 if h_ref.shape[1] % 1024 == 0 else 128

    def step(at, total):
        cut = pl.ds(pl.multiple_of(at * width, width), width)
        return squares_of(h_ref[:, cut].astype(jnp.float32), total)

    squares[...] = lax.fori_loop(0, h_ref.shape[1] // width, step, jnp.zeros(squares.shape, jnp.float32))


def stage_tokens(tokens, early):
    return pl.pallas_call(
        stage_kernel,
        out_shape=jax.ShapeDtypeStruct((tokens.shape[0], 128), jnp.float32),
        in_specs=[pl.BlockSpec(memory_space=pltpu.VMEM)] + [pl.BlockSpec(memory_space=pl.ANY)] * len(early),
        out_specs=pl.BlockSpec(memory_space=pltpu.VMEM),
        compiler_params=pltpu.CompilerParams(vmem_limit_bytes=4 * 2**20),
    )(tokens, *early)


def in_upper_half():
    return (lax.axis_index("fsdp") >= lax.axis_size("fsdp") // 2).astype(jnp.int32)


def adapter_kernel(n_arrays, sources, places, units, width, *refs):
    h0, g2, squares0 = refs[:3]
    arrays = refs[3 : 3 + n_arrays]
    outs = refs[3 + n_arrays : -2]
    w_ref, h1 = refs[-2:]
    n_pieces = len(sources)
    tokens, model_width = h0.shape
    stacked = n_pieces * ROWS // 2
    hidden = stacked // 2
    in_scale = model_width ** (-0.5)
    out_scale = hidden ** (-0.5)
    steps = model_width // 2 // width
    upper = in_upper_half()
    half = n_pieces // 2
    w_in, w_out = pl.ds(0, stacked), pl.ds(stacked, stacked)
    layer_of = (lax.broadcasted_iota(jnp.int32, (tokens, stacked), 1) % (2 * units)) // units
    no_squares = jnp.zeros((tokens, 128), jnp.float32)

    def cut(step, side=0):
        return pl.ds(pl.multiple_of(side * (model_width // 2) + step * width, width), width)

    def inv_rms(squares):
        return lax.rsqrt(jnp.sum(squares, axis=1, keepdims=True) / model_width + norm_eps)

    def first(step, total):
        low = cut(step)
        for part in range(2):
            values = []
            for k in range(part * half, part * half + half):
                array, place = sources[k]
                values.append(arrays[array][place, :, low].astype(jnp.float32))
            rows = pl.ds(pl.multiple_of((part ^ upper) * stacked, stacked), stacked)
            for side in range(2):
                block = jnp.concatenate([v[side * ROWS : (side + 1) * ROWS] for v in values])
                w_ref[rows, cut(step, side)] = block.astype(jnp.bfloat16)
        for side in range(2):
            at = cut(step, side)
            total = total + dot_nt(jnp.concatenate([h0[:, at], g2[:, at], w_ref[w_in, at]]), w_ref[:, at])
        return total

    total = jnp.zeros((2 * tokens + stacked, 2 * stacked), jnp.float32)
    total = lax.fori_loop(0, steps, first, total)
    pre0 = total[:tokens, :stacked]
    grad_act = total[tokens : 2 * tokens, stacked:]
    cross = total[2 * tokens :, stacked:]
    inv0 = inv_rms(squares0[...])
    pre0 = pre0 * (inv0 * in_scale)
    sig0 = jax.nn.sigmoid(pre0)
    act0 = jnp.where(layer_of == 0, pre0 * sig0, 0.0)
    act0_low = act0.astype(jnp.bfloat16)

    def second(step, carry):
        both, squares = carry
        for side in range(2):
            at = cut(step, side)
            out = h0[:, at].astype(jnp.float32) + dot(act0_low, w_ref[w_out, at]) * out_scale
            low = out.astype(jnp.bfloat16)
            h1[:, at] = low
            both = both + dot_nt(low, w_ref[:, at])
            squares = squares_of(low.astype(jnp.float32), squares)
        return both, squares

    both = jnp.zeros((tokens, 2 * stacked), jnp.float32)
    both, squares = lax.fori_loop(0, steps, second, (both, no_squares))
    inv1 = inv_rms(squares)
    pre1 = both[:, :stacked] * (inv1 * in_scale)
    sig1 = jax.nn.sigmoid(pre1)
    act1 = jnp.where(layer_of == 1, pre1 * sig1, 0.0)
    slope1 = sig1 * (1.0 + pre1 * (1.0 - sig1))
    gp1 = jnp.where(layer_of == 1, grad_act * out_scale * slope1, 0.0)
    gp1_low = gp1.astype(jnp.bfloat16)
    gp1 = gp1_low.astype(jnp.float32)
    coef = inv1 * inv1 * jnp.sum(gp1 * pre1, axis=1, keepdims=True) / model_width
    factor = inv1 * in_scale
    grad_act0 = grad_act + factor * dot(gp1, cross, lax.Precision.HIGHEST) - coef * both[:, stacked:]
    slope0 = sig0 * (1.0 + pre0 * (1.0 - sig0))
    gp0 = jnp.where(layer_of == 0, grad_act0 * out_scale * slope0, 0.0)
    act_t = jnp.concatenate([act0.T, act1.T], axis=1).astype(jnp.bfloat16)
    gp_t = jnp.concatenate([(gp0 * inv0).T, (gp1 * inv1).T], axis=1).astype(jnp.bfloat16)

    def third(step, carry):
        terms = []
        for side in range(2):
            at = cut(step, side)
            g1 = (
                g2[:, at].astype(jnp.float32)
                + factor * dot(gp1_low, w_ref[w_in, at])
                - coef * h1[:, at].astype(jnp.float32)
            ).astype(jnp.bfloat16)
            grad_out = dot(act_t, jnp.concatenate([g1, g2[:, at]]))
            grad_in = dot(gp_t, jnp.concatenate([h0[:, at], h1[:, at]]))
            terms.append([jnp.where(upper == part, grad_in, grad_out) for part in range(2)])
        for k in range(n_pieces):
            out, place = places[k]
            part, j = k // half, k % half
            rows = [terms[side][part][j * ROWS : (j + 1) * ROWS] for side in range(2)]
            outs[out][place, :, cut(step)] = jnp.concatenate(rows).astype(jnp.bfloat16)
        return carry

    lax.fori_loop(0, steps, third, 0)


def places_of(sets):
    return {k: (at, place) for at, ks in enumerate(sets) for place, k in enumerate(ks)}


def adapter_grads(tokens, upstream, squares, gathered, units, sets):
    model_width = tokens.shape[1]
    arrays = [array for _, array in gathered]
    sources = places_of([ks for ks, _ in gathered])
    places = places_of(sets)
    width = 1792 if model_width % 3584 == 0 else 128
    stacked = len(sources) * ROWS // 2
    whole = pl.BlockSpec(memory_space=pltpu.VMEM)
    shapes = [(len(ks), 2 * ROWS, model_width // 2) for ks in sets]
    return pl.pallas_call(
        functools.partial(adapter_kernel, len(arrays), sources, places, units, width),
        out_shape=[jax.ShapeDtypeStruct(shape, jnp.bfloat16) for shape in shapes],
        in_specs=[whole] * (3 + len(arrays)),
        out_specs=[whole] * len(sets),
        scratch_shapes=[
            pltpu.VMEM((2 * stacked, model_width), jnp.bfloat16),
            pltpu.VMEM(tokens.shape, jnp.bfloat16),
        ],
        compiler_params=pltpu.CompilerParams(vmem_limit_bytes=14 * 2**20),
    )(tokens, upstream, squares, *arrays)


def delta_kernel(fragment, params, other, anchor, total):
    chosen = lax.rem(fragment[0], params.shape[0])
    total[...] = (anchor[...] - params[chosen]) + (anchor[...] - other[chosen])


def fragment_delta(fragment, params, other, anchor):
    whole = pl.BlockSpec(memory_space=pltpu.VMEM)
    return pl.pallas_call(
        delta_kernel,
        out_shape=jax.ShapeDtypeStruct(anchor.shape, jnp.float32),
        in_specs=[pl.BlockSpec(memory_space=pltpu.SMEM)] + [whole] * 3,
        out_specs=whole,
        compiler_params=pltpu.CompilerParams(vmem_limit_bytes=2 * 2**20),
    )(fragment, params, other, anchor)


def adam_kernel(n_parts, tokens, scales, *refs):
    fragment, params, first_moment, second_moment, new_global = refs[:5]
    parts = refs[5 : 5 + n_parts]
    out, flat, merged, sem = refs[5 + n_parts :]
    layers, rows, _ = params.shape
    piece = parts[0].shape[0] // 2
    tiles = parts[0].shape[1] // 128
    scale = jnp.where(in_upper_half() == 1, scales[1] / tokens, scales[0] / tokens)
    for tile in range(tiles):
        at = pl.ds(tile * 128, 128)
        total = parts[0][:, at].astype(jnp.float32)
        for part in parts[1:]:
            total = total + part[:, at].astype(jnp.float32)
        total = total * scale
        flat[pl.ds(tile, piece, stride=2 * tiles), :] = total[:piece]
        flat[pl.ds(tiles + tile, piece, stride=2 * tiles), :] = total[piece:]
    count = jnp.full((8, 128), fragment[0], jnp.int32).astype(jnp.float32)
    correct_one = (1.0 - jnp.exp(count * math.log(beta_one)))[:1]
    correct_two = (1.0 - jnp.exp(count * math.log(beta_two)))[:1]
    chosen = lax.rem(fragment[0], layers)
    copies = []
    for layer in range(layers):
        gradient = flat[pl.ds(layer * rows, rows), :]
        moment_one = beta_one * first_moment[layer] + (1.0 - beta_one) * gradient
        moment_two = beta_two * second_moment[layer] + (1.0 - beta_two) * gradient * gradient
        updated = params[layer] - inner_rate * (
            moment_one / correct_one / (jnp.sqrt(moment_two / correct_two) + adam_eps)
            + decay_rate * params[layer]
        )
        mixed = mixing * updated + (1.0 - mixing) * new_global[...]
        merged[layer] = jnp.where(chosen == layer, mixed, updated)
        copies.append(pltpu.make_async_copy(merged.at[layer], out.at[layer], sem.at[layer]))
        copies[-1].start()
    for copy in copies:
        copy.wait()


def adam_step(fragment, params, first_moment, second_moment, new_global, parts, tokens, scales):
    whole = pl.BlockSpec(memory_space=pltpu.VMEM)
    layers, rows, lanes = params.shape
    return pl.pallas_call(
        functools.partial(adam_kernel, len(parts), tokens, scales),
        out_shape=jax.ShapeDtypeStruct(params.shape, jnp.float32),
        in_specs=[pl.BlockSpec(memory_space=pltpu.SMEM)] + [whole] * (4 + len(parts)),
        out_specs=pl.BlockSpec(memory_space=pltpu.HBM),
        scratch_shapes=[
            pltpu.VMEM((layers * rows, lanes), jnp.float32),
            pltpu.VMEM(params.shape, jnp.float32),
            pltpu.SemaphoreType.DMA((layers,)),
        ],
        compiler_params=pltpu.CompilerParams(vmem_limit_bytes=4 * 2**20),
    )(fragment, params, first_moment, second_moment, new_global, *parts)


def shards(inputs, cotangent, weights, first_moment, second_moment, anchor, momentum, fragment):
    tokens = inputs[0]
    upstream = cotangent[0]
    params = weights[0]
    layers, rows = params.shape[0], params.shape[1]
    model_width = tokens.shape[1]
    groups = lax.axis_size("fsdp")
    replicas = lax.axis_size("rep")
    units = rows * 128 // model_width
    hidden = units * groups // 2
    piece = layers * units
    compact = params.astype(jnp.bfloat16).reshape(piece, 2, model_width // 2)
    compact = compact.transpose(1, 0, 2).reshape(2 * piece, model_width // 2)
    other = swap(params, "rep", 1)
    kept = []

    def stage(blocks):
        kept.append(stage_tokens(tokens, blocks))
        return kept[0]

    gathered = gather_blocks(compact, "fsdp", stage, other)
    squares = kept[0]

    sets = output_sets(groups)
    if piece == ROWS:
        odd, even = adapter_grads(tokens, upstream, squares, gathered, units, sets)
    else:
        merged = ROWS // piece
        blocks = {k: array[place] for ks, array in gathered for place, k in enumerate(ks)}
        blocks = jnp.stack([blocks[k] for k in range(groups)])
        blocks = blocks.reshape(groups // merged, merged, 2, piece, model_width // 2)
        blocks = blocks.transpose(0, 2, 1, 3, 4).reshape(groups // merged, 2 * ROWS, model_width // 2)
        every = list(range(groups // merged))
        (both,) = adapter_grads(tokens, upstream, squares, [(every, blocks)], units, [every])
        both = both.reshape(groups // merged, 2, merged, piece, model_width // 2)
        both = both.transpose(0, 2, 1, 3, 4).reshape(groups, 2 * piece, model_width // 2)
        odd, even = [jnp.stack([both[k] for k in ks]) for ks in sets]
    parts = reduce_blocks(odd, even, "fsdp")

    total = fragment_delta(fragment, params, other, anchor)
    step = 2
    while step < replicas:
        total = total + swap(total, "rep", step)
        step *= 2
    mean_delta = after(total, parts[1]) / replicas
    new_velocity = outer_beta * momentum + mean_delta
    new_global = anchor - outer_rate * (mean_delta + outer_beta * new_velocity)
    scales = (model_width ** (-0.5), hidden ** (-0.5))
    merged = adam_step(
        fragment, params, first_moment[0], second_moment[0], new_global, parts, tokens.shape[0] * groups, scales
    )
    return (merged[None], new_global, new_velocity)


def solution(mesh):
    placed = (
        P("rep", "fsdp", None),
        P("rep", "fsdp", None),
        P("rep", None, "fsdp", None),
        P("rep", None, "fsdp", None),
        P("rep", None, "fsdp", None),
        P("fsdp", None),
        P("fsdp", None),
        P(),
    )
    return jax.shard_map(
        shards,
        mesh=mesh,
        in_specs=placed,
        out_specs=(P("rep", None, "fsdp", None), P("fsdp", None), P("fsdp", None)),
        check_vma=False,
    )
```

```python
import functools
import math

import jax
import jax.numpy as jnp
from jax import lax
from jax.experimental import pallas as pl
from jax.experimental.pallas import tpu as pltpu
from jax.sharding import PartitionSpec as P

norm_eps = 1e-05
beta_one = 0.9
beta_two = 0.95
adam_eps = 1e-08
decay_rate = 0.1
inner_rate = 0.05
outer_rate = 0.7
outer_beta = 0.9
mixing = 0.5
ROWS = 8


def swap(value, axis, mask):
    size = lax.axis_size(axis)
    return lax.ppermute(value, axis, [(i, i ^ mask) for i in range(size)])


def after(value, *others):
    return lax.optimization_barrier((value, *others))[0]


def gather_blocks(own, axis, stage, late):
    size = lax.axis_size(axis)
    single = [k for k in range(4, size, 4) if k & (k - 1) == 0]
    others = [k for k in range(4, size, 4) if k & (k - 1)]
    own = own[None]
    have = {0: own}
    for k in reversed(single):
        have[k] = swap(own, axis, k)
    near = swap(own, axis, 2)
    for k in others:
        have[k] = swap(have[k & (k - 1)], axis, k & -k)
    first = jnp.concatenate([have[k] for k in single])
    second = jnp.concatenate([have[k] for k in others])
    far_first = swap(first, axis, 2)
    second = after(second, stage((have[single[-1]],)))
    far_second = swap(second, axis, 2)
    sets = [
        ([0, 2] + single, after(jnp.concatenate([own, near, first]), late)),
        (others + [k + 2 for k in single + others], jnp.concatenate([second, far_first, far_second])),
    ]
    crossed = [([k + 1 for k in ks], swap(blocks, axis, 1)) for ks, blocks in sets]
    return sets + crossed


def add_f32(left, right):
    return left.astype(jnp.float32) + right.astype(jnp.float32)


def output_sets(size):
    tops = list(range(size - 4, -1, -4))
    even = [k + 2 for k in tops] + tops
    return [[k + 1 for k in even], even]


def reduce_blocks(odd, even, axis):
    size = lax.axis_size(axis)
    tops = list(range(size - 4, -1, -4))
    came = swap(odd, axis, 1)
    sums = add_f32(even[: len(tops)], came[: len(tops)]).astype(jnp.bfloat16)
    came = after(came, sums)
    kept = add_f32(even[len(tops) :], came[len(tops) :])
    near = [swap(sums[0], axis, 2)]
    middle = swap(after(sums[1:-1], near[0]), axis, 2)
    near += [middle[at] for at in range(len(tops) - 2)]
    left, parts = {}, []
    for at, k in enumerate(tops[:-1]):
        arrived = after(near[at], part) if at > 1 else near[at]
        part = (left.get(k, 0.0) + kept[at] + arrived.astype(jnp.float32)).astype(jnp.bfloat16)
        moved = swap(part, axis, k & -k)
        if k & (k - 1):
            left[k & (k - 1)] = left.get(k & (k - 1), 0.0) + moved.astype(jnp.float32)
        else:
            parts.append(moved)
        if at == len(tops) - 3:
            last = swap(after(sums[-1], part), axis, 2)
    return [kept[-1], last] + parts


def dot_nt(left, right):
    return lax.dot_general(left, right, (((1,), (1,)), ((), ())), preferred_element_type=jnp.float32)


def dot(left, right, precision=None):
    return jnp.dot(left, right, preferred_element_type=jnp.float32, precision=precision)


def squares_of(value, total):
    value = value * value
    for j in range(0, value.shape[1], 128):
        total = total + value[:, j : j + 128]
    return total


def stage_kernel(h_ref, *refs):
    squares = refs[-1]
    width = 1024 if h_ref.shape[1] % 1024 == 0 else 128

    def step(at, total):
        cut = pl.ds(pl.multiple_of(at * width, width), width)
        return squares_of(h_ref[:, cut].astype(jnp.float32), total)

    squares[...] = lax.fori_loop(0, h_ref.shape[1] // width, step, jnp.zeros(squares.shape, jnp.float32))


def stage_tokens(tokens, early):
    return pl.pallas_call(
        stage_kernel,
        out_shape=jax.ShapeDtypeStruct((tokens.shape[0], 128), jnp.float32),
        in_specs=[pl.BlockSpec(memory_space=pltpu.VMEM)] + [pl.BlockSpec(memory_space=pl.ANY)] * len(early),
        out_specs=pl.BlockSpec(memory_space=pltpu.VMEM),
        compiler_params=pltpu.CompilerParams(vmem_limit_bytes=4 * 2**20),
    )(tokens, *early)


def in_upper_half():
    return (lax.axis_index("fsdp") >= lax.axis_size("fsdp") // 2).astype(jnp.int32)


def adapter_kernel(n_arrays, sources, places, units, width, *refs):
    h0, g2, squares0 = refs[:3]
    arrays = refs[3 : 3 + n_arrays]
    outs = refs[3 + n_arrays : -2]
    w_ref, h1 = refs[-2:]
    n_pieces = len(sources)
    tokens, model_width = h0.shape
    stacked = n_pieces * ROWS // 2
    hidden = stacked // 2
    in_scale = model_width ** (-0.5)
    out_scale = hidden ** (-0.5)
    steps = model_width // 2 // width
    upper = in_upper_half()
    half = n_pieces // 2
    w_in, w_out = pl.ds(0, stacked), pl.ds(stacked, stacked)
    layer_of = (lax.broadcasted_iota(jnp.int32, (tokens, stacked), 1) % (2 * units)) // units
    no_squares = jnp.zeros((tokens, 128), jnp.float32)

    def cut(step, side=0):
        return pl.ds(pl.multiple_of(side * (model_width // 2) + step * width, width), width)

    def inv_rms(squares):
        return lax.rsqrt(jnp.sum(squares, axis=1, keepdims=True) / model_width + norm_eps)

    def first(step, total):
        low = cut(step)
        for part in range(2):
            values = []
            for k in range(part * half, part * half + half):
                array, place = sources[k]
                values.append(arrays[array][place, :, low].astype(jnp.float32))
            rows = pl.ds(pl.multiple_of((part ^ upper) * stacked, stacked), stacked)
            for side in range(2):
                block = jnp.concatenate([v[side * ROWS : (side + 1) * ROWS] for v in values])
                w_ref[rows, cut(step, side)] = block.astype(jnp.bfloat16)
        for side in range(2):
            at = cut(step, side)
            total = total + dot_nt(jnp.concatenate([h0[:, at], g2[:, at], w_ref[w_in, at]]), w_ref[:, at])
        return total

    total = jnp.zeros((2 * tokens + stacked, 2 * stacked), jnp.float32)
    total = lax.fori_loop(0, steps, first, total)
    pre0 = total[:tokens, :stacked]
    grad_act = total[tokens : 2 * tokens, stacked:]
    cross = total[2 * tokens :, stacked:]
    inv0 = inv_rms(squares0[...])
    pre0 = pre0 * (inv0 * in_scale)
    sig0 = jax.nn.sigmoid(pre0)
    act0 = jnp.where(layer_of == 0, pre0 * sig0, 0.0)
    act0_low = act0.astype(jnp.bfloat16)

    def second(step, carry):
        both, squares = carry
        for side in range(2):
            at = cut(step, side)
            out = h0[:, at].astype(jnp.float32) + dot(act0_low, w_ref[w_out, at]) * out_scale
            low = out.astype(jnp.bfloat16)
            h1[:, at] = low
            both = both + dot_nt(low, w_ref[:, at])
            squares = squares_of(low.astype(jnp.float32), squares)
        return both, squares

    both = jnp.zeros((tokens, 2 * stacked), jnp.float32)
    both, squares = lax.fori_loop(0, steps, second, (both, no_squares))
    inv1 = inv_rms(squares)
    pre1 = both[:, :stacked] * (inv1 * in_scale)
    sig1 = jax.nn.sigmoid(pre1)
    act1 = jnp.where(layer_of == 1, pre1 * sig1, 0.0)
    slope1 = sig1 * (1.0 + pre1 * (1.0 - sig1))
    gp1 = jnp.where(layer_of == 1, grad_act * out_scale * slope1, 0.0)
    gp1_low = gp1.astype(jnp.bfloat16)
    gp1 = gp1_low.astype(jnp.float32)
    coef = inv1 * inv1 * jnp.sum(gp1 * pre1, axis=1, keepdims=True) / model_width
    factor = inv1 * in_scale
    grad_act0 = grad_act + factor * dot(gp1, cross, lax.Precision.HIGHEST) - coef * both[:, stacked:]
    slope0 = sig0 * (1.0 + pre0 * (1.0 - sig0))
    gp0 = jnp.where(layer_of == 0, grad_act0 * out_scale * slope0, 0.0)
    act_t = jnp.concatenate([act0.T, act1.T], axis=1).astype(jnp.bfloat16)
    gp_t = jnp.concatenate([(gp0 * inv0).T, (gp1 * inv1).T], axis=1).astype(jnp.bfloat16)

    def third(step, carry):
        terms = []
        for side in range(2):
            at = cut(step, side)
            g1 = (
                g2[:, at].astype(jnp.float32)
                + factor * dot(gp1_low, w_ref[w_in, at])
                - coef * h1[:, at].astype(jnp.float32)
            ).astype(jnp.bfloat16)
            grad_out = dot(act_t, jnp.concatenate([g1, g2[:, at]]))
            grad_in = dot(gp_t, jnp.concatenate([h0[:, at], h1[:, at]]))
            terms.append([jnp.where(upper == part, grad_in, grad_out) for part in range(2)])
        for k in range(n_pieces):
            out, place = places[k]
            part, j = k // half, k % half
            rows = [terms[side][part][j * ROWS : (j + 1) * ROWS] for side in range(2)]
            outs[out][place, :, cut(step)] = jnp.concatenate(rows).astype(jnp.bfloat16)
        return carry

    lax.fori_loop(0, steps, third, 0)


def places_of(sets):
    return {k: (at, place) for at, ks in enumerate(sets) for place, k in enumerate(ks)}


def adapter_grads(tokens, upstream, squares, gathered, units, sets):
    model_width = tokens.shape[1]
    arrays = [array for _, array in gathered]
    sources = places_of([ks for ks, _ in gathered])
    places = places_of(sets)
    width = 1792 if model_width % 3584 == 0 else 128
    stacked = len(sources) * ROWS // 2
    whole = pl.BlockSpec(memory_space=pltpu.VMEM)
    shapes = [(len(ks), 2 * ROWS, model_width // 2) for ks in sets]
    return pl.pallas_call(
        functools.partial(adapter_kernel, len(arrays), sources, places, units, width),
        out_shape=[jax.ShapeDtypeStruct(shape, jnp.bfloat16) for shape in shapes],
        in_specs=[whole] * (3 + len(arrays)),
        out_specs=[whole] * len(sets),
        scratch_shapes=[
            pltpu.VMEM((2 * stacked, model_width), jnp.bfloat16),
            pltpu.VMEM(tokens.shape, jnp.bfloat16),
        ],
        compiler_params=pltpu.CompilerParams(vmem_limit_bytes=14 * 2**20),
    )(tokens, upstream, squares, *arrays)


def delta_kernel(fragment, params, other, anchor, total):
    chosen = lax.rem(fragment[0], params.shape[0])
    total[...] = (anchor[...] - params[chosen]) + (anchor[...] - other[chosen])


def fragment_delta(fragment, params, other, anchor):
    whole = pl.BlockSpec(memory_space=pltpu.VMEM)
    return pl.pallas_call(
        delta_kernel,
        out_shape=jax.ShapeDtypeStruct(anchor.shape, jnp.float32),
        in_specs=[pl.BlockSpec(memory_space=pltpu.SMEM)] + [whole] * 3,
        out_specs=whole,
        compiler_params=pltpu.CompilerParams(vmem_limit_bytes=2 * 2**20),
    )(fragment, params, other, anchor)


def adam_kernel(n_parts, tokens, scales, *refs):
    fragment, params, first_moment, second_moment, new_global = refs[:5]
    parts = refs[5 : 5 + n_parts]
    out, flat, merged, sem = refs[5 + n_parts :]
    layers, rows, _ = params.shape
    piece = parts[0].shape[0] // 2
    tiles = parts[0].shape[1] // 128
    scale = jnp.where(in_upper_half() == 1, scales[1] / tokens, scales[0] / tokens)
    for tile in range(tiles):
        at = pl.ds(tile * 128, 128)
        total = parts[0][:, at].astype(jnp.float32)
        for part in parts[1:]:
            total = total + part[:, at].astype(jnp.float32)
        total = total * scale
        flat[pl.ds(tile, piece, stride=2 * tiles), :] = total[:piece]
        flat[pl.ds(tiles + tile, piece, stride=2 * tiles), :] = total[piece:]
    count = jnp.full((8, 128), fragment[0], jnp.int32).astype(jnp.float32)
    correct_one = (1.0 - jnp.exp(count * math.log(beta_one)))[:1]
    correct_two = (1.0 - jnp.exp(count * math.log(beta_two)))[:1]
    chosen = lax.rem(fragment[0], layers)
    copies = []
    for layer in range(layers):
        gradient = flat[pl.ds(layer * rows, rows), :]
        moment_one = beta_one * first_moment[layer] + (1.0 - beta_one) * gradient
        moment_two = beta_two * second_moment[layer] + (1.0 - beta_two) * gradient * gradient
        updated = params[layer] - inner_rate * (
            moment_one / correct_one / (jnp.sqrt(moment_two / correct_two) + adam_eps)
            + decay_rate * params[layer]
        )
        mixed = mixing * updated + (1.0 - mixing) * new_global[...]
        merged[layer] = jnp.where(chosen == layer, mixed, updated)
        copies.append(pltpu.make_async_copy(merged.at[layer], out.at[layer], sem.at[layer]))
        copies[-1].start()
    for copy in copies:
        copy.wait()


def adam_step(fragment, params, first_moment, second_moment, new_global, parts, tokens, scales):
    whole = pl.BlockSpec(memory_space=pltpu.VMEM)
    layers, rows, lanes = params.shape
    return pl.pallas_call(
        functools.partial(adam_kernel, len(parts), tokens, scales),
        out_shape=jax.ShapeDtypeStruct(params.shape, jnp.float32),
        in_specs=[pl.BlockSpec(memory_space=pltpu.SMEM)] + [whole] * (4 + len(parts)),
        out_specs=pl.BlockSpec(memory_space=pltpu.HBM),
        scratch_shapes=[
            pltpu.VMEM((layers * rows, lanes), jnp.float32),
            pltpu.VMEM(params.shape, jnp.float32),
            pltpu.SemaphoreType.DMA((layers,)),
        ],
        compiler_params=pltpu.CompilerParams(vmem_limit_bytes=4 * 2**20),
    )(fragment, params, first_moment, second_moment, new_global, *parts)


def shards(inputs, cotangent, weights, first_moment, second_moment, anchor, momentum, fragment):
    tokens = inputs[0]
    upstream = cotangent[0]
    params = weights[0]
    layers, rows = params.shape[0], params.shape[1]
    model_width = tokens.shape[1]
    groups = lax.axis_size("fsdp")
    replicas = lax.axis_size("rep")
    units = rows * 128 // model_width
    hidden = units * groups // 2
    piece = layers * units
    compact = params.astype(jnp.bfloat16).reshape(piece, 2, model_width // 2)
    compact = compact.transpose(1, 0, 2).reshape(2 * piece, model_width // 2)
    other = swap(params, "rep", 1)
    kept = []

    def stage(blocks):
        kept.append(stage_tokens(tokens, blocks))
        return kept[0]

    gathered = gather_blocks(compact, "fsdp", stage, other)
    squares = kept[0]

    sets = output_sets(groups)
    if piece == ROWS:
        odd, even = adapter_grads(tokens, upstream, squares, gathered, units, sets)
    else:
        merged = ROWS // piece
        blocks = {k: array[place] for ks, array in gathered for place, k in enumerate(ks)}
        blocks = jnp.stack([blocks[k] for k in range(groups)])
        blocks = blocks.reshape(groups // merged, merged, 2, piece, model_width // 2)
        blocks = blocks.transpose(0, 2, 1, 3, 4).reshape(groups // merged, 2 * ROWS, model_width // 2)
        every = list(range(groups // merged))
        (both,) = adapter_grads(tokens, upstream, squares, [(every, blocks)], units, [every])
        both = both.reshape(groups // merged, 2, merged, piece, model_width // 2)
        both = both.transpose(0, 2, 1, 3, 4).reshape(groups, 2 * piece, model_width // 2)
        odd, even = [jnp.stack([both[k] for k in ks]) for ks in sets]
    parts = reduce_blocks(odd, even, "fsdp")

    total = fragment_delta(fragment, params, other, anchor)
    step = 2
    while step < replicas:
        total = total + swap(total, "rep", step)
        step *= 2
    mean_delta = after(total, parts[-1]) / replicas
    new_velocity = outer_beta * momentum + mean_delta
    new_global = anchor - outer_rate * (mean_delta + outer_beta * new_velocity)
    scales = (model_width ** (-0.5), hidden ** (-0.5))
    merged = adam_step(
        fragment, params, first_moment[0], second_moment[0], new_global, parts, tokens.shape[0] * groups, scales
    )
    return (merged[None], new_global, new_velocity)


def solution(mesh):
    placed = (
        P("rep", "fsdp", None),
        P("rep", "fsdp", None),
        P("rep", None, "fsdp", None),
        P("rep", None, "fsdp", None),
        P("rep", None, "fsdp", None),
        P("fsdp", None),
        P("fsdp", None),
        P(),
    )
    return jax.shard_map(
        shards,
        mesh=mesh,
        in_specs=placed,
        out_specs=(P("rep", None, "fsdp", None), P("fsdp", None), P("fsdp", None)),
        check_vma=False,
    )
```

```python
import functools
import math

import jax
import jax.numpy as jnp
from jax import lax
from jax.experimental import pallas as pl
from jax.experimental.pallas import tpu as pltpu
from jax.sharding import PartitionSpec as P

norm_eps = 1e-05
beta_one = 0.9
beta_two = 0.95
adam_eps = 1e-08
decay_rate = 0.1
inner_rate = 0.05
outer_rate = 0.7
outer_beta = 0.9
mixing = 0.5
ROWS = 8


def swap(value, axis, mask):
    size = lax.axis_size(axis)
    return lax.ppermute(value, axis, [(i, i ^ mask) for i in range(size)])


def after(value, *others):
    return lax.optimization_barrier((value, *others))[0]


def gather_blocks(own, axis, stage, late):
    size = lax.axis_size(axis)
    single = [k for k in range(4, size, 4) if k & (k - 1) == 0]
    others = [k for k in range(4, size, 4) if k & (k - 1)]
    own = own[None]
    have = {0: own}
    for k in reversed(single):
        have[k] = swap(own, axis, k)
    near = swap(own, axis, 2)
    for k in others:
        have[k] = swap(have[k & (k - 1)], axis, k & -k)
    first = jnp.concatenate([have[k] for k in single])
    second = jnp.concatenate([have[k] for k in others])
    far_first = swap(first, axis, 2)
    second = after(second, stage((have[single[-1]],)))
    far_second = swap(second, axis, 2)
    sets = [
        ([0, 2] + single, after(jnp.concatenate([own, near, first]), late)),
        (others + [k + 2 for k in single + others], jnp.concatenate([second, far_first, far_second])),
    ]
    crossed = [([k + 1 for k in ks], swap(blocks, axis, 1)) for ks, blocks in sets]
    return sets + crossed


def add_f32(left, right):
    return left.astype(jnp.float32) + right.astype(jnp.float32)


def output_sets(size):
    tops = list(range(size - 4, -1, -4))
    half = len(tops) // 2
    parts = [[k + 2 for k in tops[:half]], [k + 2 for k in tops[half:]], tops]
    return [[k + 1 for k in ks] for ks in parts] + parts


def reduce_blocks(outs, axis):
    size = lax.axis_size(axis)
    tops = list(range(size - 4, -1, -4))
    half = len(tops) // 2
    came = swap(outs[0], axis, 1)
    sums = add_f32(outs[3], came).astype(jnp.bfloat16)
    near = [swap(sums[at], axis, 2) for at in range(half)]
    odd, last_odd, sums = lax.optimization_barrier((outs[1], outs[2], sums))
    came = swap(odd, axis, 1)
    sums = add_f32(outs[4], came).astype(jnp.bfloat16)
    rest = swap(sums, axis, 2)
    near[0] = after(near[0], sums)
    kept = add_f32(outs[5], swap(last_odd, axis, 1))
    left = {}
    for at, k in enumerate(tops):
        if at == half:
            rest = after(rest, part)
        arrived = near[at] if at < half else rest[at - half]
        left[k] = left.get(k, 0.0) + kept[at] + arrived.astype(jnp.float32)
        if k:
            part = left[k].astype(jnp.bfloat16)
            moved = swap(part, axis, k & -k).astype(jnp.float32)
            left[k & (k - 1)] = left.get(k & (k - 1), 0.0) + moved
    return left[0]


def dot_nt(left, right):
    return lax.dot_general(left, right, (((1,), (1,)), ((), ())), preferred_element_type=jnp.float32)


def dot(left, right, precision=None):
    return jnp.dot(left, right, preferred_element_type=jnp.float32, precision=precision)


def squares_of(value, total):
    value = value * value
    for j in range(0, value.shape[1], 128):
        total = total + value[:, j : j + 128]
    return total


def stage_kernel(h_ref, *refs):
    squares = refs[-1]
    width = 1024 if h_ref.shape[1] % 1024 == 0 else 128

    def step(at, total):
        cut = pl.ds(pl.multiple_of(at * width, width), width)
        return squares_of(h_ref[:, cut].astype(jnp.float32), total)

    squares[...] = lax.fori_loop(0, h_ref.shape[1] // width, step, jnp.zeros(squares.shape, jnp.float32))


def stage_tokens(tokens, early):
    return pl.pallas_call(
        stage_kernel,
        out_shape=jax.ShapeDtypeStruct((tokens.shape[0], 128), jnp.float32),
        in_specs=[pl.BlockSpec(memory_space=pltpu.VMEM)] + [pl.BlockSpec(memory_space=pl.ANY)] * len(early),
        out_specs=pl.BlockSpec(memory_space=pltpu.VMEM),
        compiler_params=pltpu.CompilerParams(vmem_limit_bytes=4 * 2**20),
    )(tokens, *early)


def in_upper_half():
    return (lax.axis_index("fsdp") >= lax.axis_size("fsdp") // 2).astype(jnp.int32)


def adapter_kernel(n_arrays, sources, places, units, width, *refs):
    h0, g2, squares0 = refs[:3]
    arrays = refs[3 : 3 + n_arrays]
    outs = refs[3 + n_arrays : -2]
    w_ref, h1 = refs[-2:]
    n_pieces = len(sources)
    tokens, model_width = h0.shape
    stacked = n_pieces * ROWS // 2
    hidden = stacked // 2
    in_scale = model_width ** (-0.5)
    out_scale = hidden ** (-0.5)
    steps = model_width // 2 // width
    upper = in_upper_half()
    half = n_pieces // 2
    w_in, w_out = pl.ds(0, stacked), pl.ds(stacked, stacked)
    layer_of = (lax.broadcasted_iota(jnp.int32, (tokens, stacked), 1) % (2 * units)) // units
    no_squares = jnp.zeros((tokens, 128), jnp.float32)

    def cut(step, side=0):
        return pl.ds(pl.multiple_of(side * (model_width // 2) + step * width, width), width)

    def inv_rms(squares):
        return lax.rsqrt(jnp.sum(squares, axis=1, keepdims=True) / model_width + norm_eps)

    def first(step, total):
        low = cut(step)
        for part in range(2):
            values = []
            for k in range(part * half, part * half + half):
                array, place = sources[k]
                values.append(arrays[array][place, :, low].astype(jnp.float32))
            rows = pl.ds(pl.multiple_of((part ^ upper) * stacked, stacked), stacked)
            for side in range(2):
                block = jnp.concatenate([v[side * ROWS : (side + 1) * ROWS] for v in values])
                w_ref[rows, cut(step, side)] = block.astype(jnp.bfloat16)
        for side in range(2):
            at = cut(step, side)
            total = total + dot_nt(jnp.concatenate([h0[:, at], g2[:, at], w_ref[w_in, at]]), w_ref[:, at])
        return total

    total = jnp.zeros((2 * tokens + stacked, 2 * stacked), jnp.float32)
    total = lax.fori_loop(0, steps, first, total)
    pre0 = total[:tokens, :stacked]
    grad_act = total[tokens : 2 * tokens, stacked:]
    cross = total[2 * tokens :, stacked:]
    inv0 = inv_rms(squares0[...])
    pre0 = pre0 * (inv0 * in_scale)
    sig0 = jax.nn.sigmoid(pre0)
    act0 = jnp.where(layer_of == 0, pre0 * sig0, 0.0)
    act0_low = act0.astype(jnp.bfloat16)

    def second(step, carry):
        both, squares = carry
        for side in range(2):
            at = cut(step, side)
            out = h0[:, at].astype(jnp.float32) + dot(act0_low, w_ref[w_out, at]) * out_scale
            low = out.astype(jnp.bfloat16)
            h1[:, at] = low
            both = both + dot_nt(low, w_ref[:, at])
            squares = squares_of(low.astype(jnp.float32), squares)
        return both, squares

    both = jnp.zeros((tokens, 2 * stacked), jnp.float32)
    both, squares = lax.fori_loop(0, steps, second, (both, no_squares))
    inv1 = inv_rms(squares)
    pre1 = both[:, :stacked] * (inv1 * in_scale)
    sig1 = jax.nn.sigmoid(pre1)
    act1 = jnp.where(layer_of == 1, pre1 * sig1, 0.0)
    slope1 = sig1 * (1.0 + pre1 * (1.0 - sig1))
    gp1 = jnp.where(layer_of == 1, grad_act * out_scale * slope1, 0.0)
    gp1_low = gp1.astype(jnp.bfloat16)
    gp1 = gp1_low.astype(jnp.float32)
    coef = inv1 * inv1 * jnp.sum(gp1 * pre1, axis=1, keepdims=True) / model_width
    factor = inv1 * in_scale
    grad_act0 = grad_act + factor * dot(gp1, cross, lax.Precision.HIGHEST) - coef * both[:, stacked:]
    slope0 = sig0 * (1.0 + pre0 * (1.0 - sig0))
    gp0 = jnp.where(layer_of == 0, grad_act0 * out_scale * slope0, 0.0)
    act_t = jnp.concatenate([act0.T, act1.T], axis=1).astype(jnp.bfloat16)
    gp_t = jnp.concatenate([(gp0 * inv0).T, (gp1 * inv1).T], axis=1).astype(jnp.bfloat16)

    def third(step, carry):
        terms = []
        for side in range(2):
            at = cut(step, side)
            g1 = (
                g2[:, at].astype(jnp.float32)
                + factor * dot(gp1_low, w_ref[w_in, at])
                - coef * h1[:, at].astype(jnp.float32)
            ).astype(jnp.bfloat16)
            grad_out = dot(act_t, jnp.concatenate([g1, g2[:, at]]))
            grad_in = dot(gp_t, jnp.concatenate([h0[:, at], h1[:, at]]))
            terms.append([jnp.where(upper == part, grad_in, grad_out) for part in range(2)])
        for k in range(n_pieces):
            out, place = places[k]
            part, j = k // half, k % half
            rows = [terms[side][part][j * ROWS : (j + 1) * ROWS] for side in range(2)]
            outs[out][place, :, cut(step)] = jnp.concatenate(rows).astype(jnp.bfloat16)
        return carry

    lax.fori_loop(0, steps, third, 0)


def places_of(sets):
    return {k: (at, place) for at, ks in enumerate(sets) for place, k in enumerate(ks)}


def adapter_grads(tokens, upstream, squares, gathered, units, sets):
    model_width = tokens.shape[1]
    arrays = [array for _, array in gathered]
    sources = places_of([ks for ks, _ in gathered])
    places = places_of(sets)
    width = 1792 if model_width % 3584 == 0 else 128
    stacked = len(sources) * ROWS // 2
    whole = pl.BlockSpec(memory_space=pltpu.VMEM)
    shapes = [(len(ks), 2 * ROWS, model_width // 2) for ks in sets]
    return pl.pallas_call(
        functools.partial(adapter_kernel, len(arrays), sources, places, units, width),
        out_shape=[jax.ShapeDtypeStruct(shape, jnp.bfloat16) for shape in shapes],
        in_specs=[whole] * (3 + len(arrays)),
        out_specs=[whole] * len(sets),
        scratch_shapes=[
            pltpu.VMEM((2 * stacked, model_width), jnp.bfloat16),
            pltpu.VMEM(tokens.shape, jnp.bfloat16),
        ],
        compiler_params=pltpu.CompilerParams(vmem_limit_bytes=14 * 2**20),
    )(tokens, upstream, squares, *arrays)


def delta_kernel(fragment, params, other, anchor, total):
    chosen = lax.rem(fragment[0], params.shape[0])
    total[...] = (anchor[...] - params[chosen]) + (anchor[...] - other[chosen])


def fragment_delta(fragment, params, other, anchor):
    whole = pl.BlockSpec(memory_space=pltpu.VMEM)
    return pl.pallas_call(
        delta_kernel,
        out_shape=jax.ShapeDtypeStruct(anchor.shape, jnp.float32),
        in_specs=[pl.BlockSpec(memory_space=pltpu.SMEM)] + [whole] * 3,
        out_specs=whole,
        compiler_params=pltpu.CompilerParams(vmem_limit_bytes=2 * 2**20),
    )(fragment, params, other, anchor)


def adam_kernel(n_parts, tokens, scales, *refs):
    fragment, params, first_moment, second_moment, new_global = refs[:5]
    parts = refs[5 : 5 + n_parts]
    out, flat, merged, sem = refs[5 + n_parts :]
    layers, rows, _ = params.shape
    piece = parts[0].shape[0] // 2
    tiles = parts[0].shape[1] // 128
    scale = jnp.where(in_upper_half() == 1, scales[1] / tokens, scales[0] / tokens)
    for tile in range(tiles):
        at = pl.ds(tile * 128, 128)
        total = parts[0][:, at].astype(jnp.float32)
        for part in parts[1:]:
            total = total + part[:, at].astype(jnp.float32)
        total = total * scale
        flat[pl.ds(tile, piece, stride=2 * tiles), :] = total[:piece]
        flat[pl.ds(tiles + tile, piece, stride=2 * tiles), :] = total[piece:]
    count = jnp.full((8, 128), fragment[0], jnp.int32).astype(jnp.float32)
    correct_one = (1.0 - jnp.exp(count * math.log(beta_one)))[:1]
    correct_two = (1.0 - jnp.exp(count * math.log(beta_two)))[:1]
    chosen = lax.rem(fragment[0], layers)
    copies = []
    for layer in range(layers):
        gradient = flat[pl.ds(layer * rows, rows), :]
        moment_one = beta_one * first_moment[layer] + (1.0 - beta_one) * gradient
        moment_two = beta_two * second_moment[layer] + (1.0 - beta_two) * gradient * gradient
        updated = params[layer] - inner_rate * (
            moment_one / correct_one / (jnp.sqrt(moment_two / correct_two) + adam_eps)
            + decay_rate * params[layer]
        )
        mixed = mixing * updated + (1.0 - mixing) * new_global[...]
        merged[layer] = jnp.where(chosen == layer, mixed, updated)
        copies.append(pltpu.make_async_copy(merged.at[layer], out.at[layer], sem.at[layer]))
        copies[-1].start()
    for copy in copies:
        copy.wait()


def adam_step(fragment, params, first_moment, second_moment, new_global, parts, tokens, scales):
    whole = pl.BlockSpec(memory_space=pltpu.VMEM)
    layers, rows, lanes = params.shape
    return pl.pallas_call(
        functools.partial(adam_kernel, len(parts), tokens, scales),
        out_shape=jax.ShapeDtypeStruct(params.shape, jnp.float32),
        in_specs=[pl.BlockSpec(memory_space=pltpu.SMEM)] + [whole] * (4 + len(parts)),
        out_specs=pl.BlockSpec(memory_space=pltpu.HBM),
        scratch_shapes=[
            pltpu.VMEM((layers * rows, lanes), jnp.float32),
            pltpu.VMEM(params.shape, jnp.float32),
            pltpu.SemaphoreType.DMA((layers,)),
        ],
        compiler_params=pltpu.CompilerParams(vmem_limit_bytes=4 * 2**20),
    )(fragment, params, first_moment, second_moment, new_global, *parts)


def shards(inputs, cotangent, weights, first_moment, second_moment, anchor, momentum, fragment):
    tokens = inputs[0]
    upstream = cotangent[0]
    params = weights[0]
    layers, rows = params.shape[0], params.shape[1]
    model_width = tokens.shape[1]
    groups = lax.axis_size("fsdp")
    replicas = lax.axis_size("rep")
    units = rows * 128 // model_width
    hidden = units * groups // 2
    piece = layers * units
    compact = params.astype(jnp.bfloat16).reshape(piece, 2, model_width // 2)
    compact = compact.transpose(1, 0, 2).reshape(2 * piece, model_width // 2)
    other = swap(params, "rep", 1)
    kept = []

    def stage(blocks):
        kept.append(stage_tokens(tokens, blocks))
        return kept[0]

    gathered = gather_blocks(compact, "fsdp", stage, other)
    squares = kept[0]

    sets = output_sets(groups)
    if piece == ROWS:
        outs = adapter_grads(tokens, upstream, squares, gathered, units, sets)
    else:
        merged = ROWS // piece
        blocks = {k: array[place] for ks, array in gathered for place, k in enumerate(ks)}
        blocks = jnp.stack([blocks[k] for k in range(groups)])
        blocks = blocks.reshape(groups // merged, merged, 2, piece, model_width // 2)
        blocks = blocks.transpose(0, 2, 1, 3, 4).reshape(groups // merged, 2 * ROWS, model_width // 2)
        every = list(range(groups // merged))
        (both,) = adapter_grads(tokens, upstream, squares, [(every, blocks)], units, [every])
        both = both.reshape(groups // merged, 2, merged, piece, model_width // 2)
        both = both.transpose(0, 2, 1, 3, 4).reshape(groups, 2 * piece, model_width // 2)
        outs = [jnp.stack([both[k] for k in ks]) for ks in sets]
    summed = reduce_blocks(outs, "fsdp")

    total = fragment_delta(fragment, params, other, anchor)
    step = 2
    while step < replicas:
        total = total + swap(total, "rep", step)
        step *= 2
    mean_delta = total / replicas
    new_velocity = outer_beta * momentum + mean_delta
    new_global = anchor - outer_rate * (mean_delta + outer_beta * new_velocity)
    scales = (model_width ** (-0.5), hidden ** (-0.5))
    merged = adam_step(
        fragment, params, first_moment[0], second_moment[0], new_global, [summed], tokens.shape[0] * groups, scales
    )
    return (merged[None], new_global, new_velocity)


def solution(mesh):
    placed = (
        P("rep", "fsdp", None),
        P("rep", "fsdp", None),
        P("rep", None, "fsdp", None),
        P("rep", None, "fsdp", None),
        P("rep", None, "fsdp", None),
        P("fsdp", None),
        P("fsdp", None),
        P(),
    )
    return jax.shard_map(
        shards,
        mesh=mesh,
        in_specs=placed,
        out_specs=(P("rep", None, "fsdp", None), P("fsdp", None), P("fsdp", None)),
        check_vma=False,
    )
```

```python
import functools
import math

import jax
import jax.numpy as jnp
from jax import lax
from jax.experimental import pallas as pl
from jax.experimental.pallas import tpu as pltpu
from jax.sharding import PartitionSpec as P

norm_eps = 1e-05
beta_one = 0.9
beta_two = 0.95
adam_eps = 1e-08
decay_rate = 0.1
inner_rate = 0.05
outer_rate = 0.7
outer_beta = 0.9
mixing = 0.5
ROWS = 8


def swap(value, axis, mask):
    size = lax.axis_size(axis)
    return lax.ppermute(value, axis, [(i, i ^ mask) for i in range(size)])


def after(value, *others):
    return lax.optimization_barrier((value, *others))[0]


def gather_blocks(own, axis, stage, late):
    size = lax.axis_size(axis)
    single = [k for k in range(4, size, 4) if k & (k - 1) == 0]
    others = [k for k in range(4, size, 4) if k & (k - 1)]
    own = own[None]
    have = {0: own}
    for k in reversed(single):
        have[k] = swap(own, axis, k)
    near = swap(own, axis, 2)
    for k in others:
        have[k] = swap(have[k & (k - 1)], axis, k & -k)
    first = jnp.concatenate([have[k] for k in single])
    second = jnp.concatenate([have[k] for k in others])
    far_first = swap(first, axis, 2)
    second = after(second, stage((have[single[-1]],)))
    far_second = swap(second, axis, 2)
    sets = [
        ([0, 2] + single, after(jnp.concatenate([own, near, first]), late)),
        (others + [k + 2 for k in single + others], jnp.concatenate([second, far_first, far_second])),
    ]
    crossed = [([k + 1 for k in ks], swap(blocks, axis, 1)) for ks, blocks in sets]
    return sets + crossed


def add_f32(left, right):
    return left.astype(jnp.float32) + right.astype(jnp.float32)


def output_sets(size):
    tops = list(range(size - 4, -1, -4))
    half = len(tops) // 2
    parts = [[k + 2 for k in tops[:half]], [k + 2 for k in tops[half:]], tops]
    return [[k + 1 for k in ks] for ks in parts] + parts


def reduce_blocks(outs, axis):
    size = lax.axis_size(axis)
    tops = list(range(size - 4, -1, -4))
    half = len(tops) // 2
    came = swap(outs[0], axis, 1)
    sums = add_f32(outs[3], came).astype(jnp.bfloat16)
    near = [swap(sums[at], axis, 2) for at in range(half)]
    odd, last_odd, sums = lax.optimization_barrier((outs[1], outs[2], sums))
    came = swap(odd, axis, 1)
    sums = add_f32(outs[4], came).astype(jnp.bfloat16)
    rest = swap(sums, axis, 2)
    near[0] = after(near[0], sums)
    kept = add_f32(outs[5], swap(last_odd, axis, 1))
    left = {}
    for at, k in enumerate(tops):
        if at == half:
            rest = after(rest, part)
        arrived = near[at] if at < half else rest[at - half]
        left[k] = left.get(k, 0.0) + kept[at] + arrived.astype(jnp.float32)
        if k:
            part = left[k].astype(jnp.bfloat16)
            moved = swap(part, axis, k & -k).astype(jnp.float32)
            left[k & (k - 1)] = left.get(k & (k - 1), 0.0) + moved
    return left[0], rest


def dot_nt(left, right):
    return lax.dot_general(left, right, (((1,), (1,)), ((), ())), preferred_element_type=jnp.float32)


def dot(left, right, precision=None):
    return jnp.dot(left, right, preferred_element_type=jnp.float32, precision=precision)


def squares_of(value, total):
    value = value * value
    for j in range(0, value.shape[1], 128):
        total = total + value[:, j : j + 128]
    return total


def stage_kernel(h_ref, *refs):
    squares = refs[-1]
    width = 1024 if h_ref.shape[1] % 1024 == 0 else 128

    def step(at, total):
        cut = pl.ds(pl.multiple_of(at * width, width), width)
        return squares_of(h_ref[:, cut].astype(jnp.float32), total)

    squares[...] = lax.fori_loop(0, h_ref.shape[1] // width, step, jnp.zeros(squares.shape, jnp.float32))


def stage_tokens(tokens, early):
    return pl.pallas_call(
        stage_kernel,
        out_shape=jax.ShapeDtypeStruct((tokens.shape[0], 128), jnp.float32),
        in_specs=[pl.BlockSpec(memory_space=pltpu.VMEM)] + [pl.BlockSpec(memory_space=pl.ANY)] * len(early),
        out_specs=pl.BlockSpec(memory_space=pltpu.VMEM),
        compiler_params=pltpu.CompilerParams(vmem_limit_bytes=4 * 2**20),
    )(tokens, *early)


def in_upper_half():
    return (lax.axis_index("fsdp") >= lax.axis_size("fsdp") // 2).astype(jnp.int32)


def adapter_kernel(n_arrays, sources, places, units, width, *refs):
    h0, g2, squares0 = refs[:3]
    arrays = refs[3 : 3 + n_arrays]
    outs = refs[3 + n_arrays : -2]
    w_ref, h1 = refs[-2:]
    n_pieces = len(sources)
    tokens, model_width = h0.shape
    stacked = n_pieces * ROWS // 2
    hidden = stacked // 2
    in_scale = model_width ** (-0.5)
    out_scale = hidden ** (-0.5)
    steps = model_width // 2 // width
    upper = in_upper_half()
    half = n_pieces // 2
    w_in, w_out = pl.ds(0, stacked), pl.ds(stacked, stacked)
    layer_of = (lax.broadcasted_iota(jnp.int32, (tokens, stacked), 1) % (2 * units)) // units
    no_squares = jnp.zeros((tokens, 128), jnp.float32)

    def cut(step, side=0):
        return pl.ds(pl.multiple_of(side * (model_width // 2) + step * width, width), width)

    def inv_rms(squares):
        return lax.rsqrt(jnp.sum(squares, axis=1, keepdims=True) / model_width + norm_eps)

    def first(step, total):
        low = cut(step)
        for part in range(2):
            values = []
            for k in range(part * half, part * half + half):
                array, place = sources[k]
                values.append(arrays[array][place, :, low].astype(jnp.float32))
            rows = pl.ds(pl.multiple_of((part ^ upper) * stacked, stacked), stacked)
            for side in range(2):
                block = jnp.concatenate([v[side * ROWS : (side + 1) * ROWS] for v in values])
                w_ref[rows, cut(step, side)] = block.astype(jnp.bfloat16)
        for side in range(2):
            at = cut(step, side)
            total = total + dot_nt(jnp.concatenate([h0[:, at], g2[:, at], w_ref[w_in, at]]), w_ref[:, at])
        return total

    total = jnp.zeros((2 * tokens + stacked, 2 * stacked), jnp.float32)
    total = lax.fori_loop(0, steps, first, total)
    pre0 = total[:tokens, :stacked]
    grad_act = total[tokens : 2 * tokens, stacked:]
    cross = total[2 * tokens :, stacked:]
    inv0 = inv_rms(squares0[...])
    pre0 = pre0 * (inv0 * in_scale)
    sig0 = jax.nn.sigmoid(pre0)
    act0 = jnp.where(layer_of == 0, pre0 * sig0, 0.0)
    act0_low = act0.astype(jnp.bfloat16)

    def second(step, carry):
        both, squares = carry
        for side in range(2):
            at = cut(step, side)
            out = h0[:, at].astype(jnp.float32) + dot(act0_low, w_ref[w_out, at]) * out_scale
            low = out.astype(jnp.bfloat16)
            h1[:, at] = low
            both = both + dot_nt(low, w_ref[:, at])
            squares = squares_of(low.astype(jnp.float32), squares)
        return both, squares

    both = jnp.zeros((tokens, 2 * stacked), jnp.float32)
    both, squares = lax.fori_loop(0, steps, second, (both, no_squares))
    inv1 = inv_rms(squares)
    pre1 = both[:, :stacked] * (inv1 * in_scale)
    sig1 = jax.nn.sigmoid(pre1)
    act1 = jnp.where(layer_of == 1, pre1 * sig1, 0.0)
    slope1 = sig1 * (1.0 + pre1 * (1.0 - sig1))
    gp1 = jnp.where(layer_of == 1, grad_act * out_scale * slope1, 0.0)
    gp1_low = gp1.astype(jnp.bfloat16)
    gp1 = gp1_low.astype(jnp.float32)
    coef = inv1 * inv1 * jnp.sum(gp1 * pre1, axis=1, keepdims=True) / model_width
    factor = inv1 * in_scale
    grad_act0 = grad_act + factor * dot(gp1, cross, lax.Precision.HIGHEST) - coef * both[:, stacked:]
    slope0 = sig0 * (1.0 + pre0 * (1.0 - sig0))
    gp0 = jnp.where(layer_of == 0, grad_act0 * out_scale * slope0, 0.0)
    act_t = jnp.concatenate([act0.T, act1.T], axis=1).astype(jnp.bfloat16)
    gp_t = jnp.concatenate([(gp0 * inv0).T, (gp1 * inv1).T], axis=1).astype(jnp.bfloat16)

    def third(step, carry):
        terms = []
        for side in range(2):
            at = cut(step, side)
            g1 = (
                g2[:, at].astype(jnp.float32)
                + factor * dot(gp1_low, w_ref[w_in, at])
                - coef * h1[:, at].astype(jnp.float32)
            ).astype(jnp.bfloat16)
            grad_out = dot(act_t, jnp.concatenate([g1, g2[:, at]]))
            grad_in = dot(gp_t, jnp.concatenate([h0[:, at], h1[:, at]]))
            terms.append([jnp.where(upper == part, grad_in, grad_out) for part in range(2)])
        for k in range(n_pieces):
            out, place = places[k]
            part, j = k // half, k % half
            rows = [terms[side][part][j * ROWS : (j + 1) * ROWS] for side in range(2)]
            outs[out][place, :, cut(step)] = jnp.concatenate(rows).astype(jnp.bfloat16)
        return carry

    lax.fori_loop(0, steps, third, 0)


def places_of(sets):
    return {k: (at, place) for at, ks in enumerate(sets) for place, k in enumerate(ks)}


def adapter_grads(tokens, upstream, squares, gathered, units, sets):
    model_width = tokens.shape[1]
    arrays = [array for _, array in gathered]
    sources = places_of([ks for ks, _ in gathered])
    places = places_of(sets)
    width = 1792 if model_width % 3584 == 0 else 128
    stacked = len(sources) * ROWS // 2
    whole = pl.BlockSpec(memory_space=pltpu.VMEM)
    shapes = [(len(ks), 2 * ROWS, model_width // 2) for ks in sets]
    return pl.pallas_call(
        functools.partial(adapter_kernel, len(arrays), sources, places, units, width),
        out_shape=[jax.ShapeDtypeStruct(shape, jnp.bfloat16) for shape in shapes],
        in_specs=[whole] * (3 + len(arrays)),
        out_specs=[whole] * len(sets),
        scratch_shapes=[
            pltpu.VMEM((2 * stacked, model_width), jnp.bfloat16),
            pltpu.VMEM(tokens.shape, jnp.bfloat16),
        ],
        compiler_params=pltpu.CompilerParams(vmem_limit_bytes=14 * 2**20),
    )(tokens, upstream, squares, *arrays)


def delta_kernel(fragment, params, other, anchor, total):
    chosen = lax.rem(fragment[0], params.shape[0])
    total[...] = (anchor[...] - params[chosen]) + (anchor[...] - other[chosen])


def fragment_delta(fragment, params, other, anchor):
    whole = pl.BlockSpec(memory_space=pltpu.VMEM)
    return pl.pallas_call(
        delta_kernel,
        out_shape=jax.ShapeDtypeStruct(anchor.shape, jnp.float32),
        in_specs=[pl.BlockSpec(memory_space=pltpu.SMEM)] + [whole] * 3,
        out_specs=whole,
        compiler_params=pltpu.CompilerParams(vmem_limit_bytes=2 * 2**20),
    )(fragment, params, other, anchor)


def adam_kernel(n_parts, tokens, scales, *refs):
    fragment, params, first_moment, second_moment, new_global = refs[:5]
    parts = refs[5 : 5 + n_parts]
    out, flat, merged, sem = refs[5 + n_parts :]
    layers, rows, _ = params.shape
    piece = parts[0].shape[0] // 2
    tiles = parts[0].shape[1] // 128
    scale = jnp.where(in_upper_half() == 1, scales[1] / tokens, scales[0] / tokens)
    for tile in range(tiles):
        at = pl.ds(tile * 128, 128)
        total = parts[0][:, at].astype(jnp.float32)
        for part in parts[1:]:
            total = total + part[:, at].astype(jnp.float32)
        total = total * scale
        flat[pl.ds(tile, piece, stride=2 * tiles), :] = total[:piece]
        flat[pl.ds(tiles + tile, piece, stride=2 * tiles), :] = total[piece:]
    count = jnp.full((8, 128), fragment[0], jnp.int32).astype(jnp.float32)
    correct_one = (1.0 - jnp.exp(count * math.log(beta_one)))[:1]
    correct_two = (1.0 - jnp.exp(count * math.log(beta_two)))[:1]
    chosen = lax.rem(fragment[0], layers)
    copies = []
    for layer in range(layers):
        gradient = flat[pl.ds(layer * rows, rows), :]
        moment_one = beta_one * first_moment[layer] + (1.0 - beta_one) * gradient
        moment_two = beta_two * second_moment[layer] + (1.0 - beta_two) * gradient * gradient
        updated = params[layer] - inner_rate * (
            moment_one / correct_one / (jnp.sqrt(moment_two / correct_two) + adam_eps)
            + decay_rate * params[layer]
        )
        mixed = mixing * updated + (1.0 - mixing) * new_global[...]
        merged[layer] = jnp.where(chosen == layer, mixed, updated)
        copies.append(pltpu.make_async_copy(merged.at[layer], out.at[layer], sem.at[layer]))
        copies[-1].start()
    for copy in copies:
        copy.wait()


def adam_step(fragment, params, first_moment, second_moment, new_global, parts, tokens, scales):
    whole = pl.BlockSpec(memory_space=pltpu.VMEM)
    layers, rows, lanes = params.shape
    return pl.pallas_call(
        functools.partial(adam_kernel, len(parts), tokens, scales),
        out_shape=jax.ShapeDtypeStruct(params.shape, jnp.float32),
        in_specs=[pl.BlockSpec(memory_space=pltpu.SMEM)] + [whole] * (4 + len(parts)),
        out_specs=pl.BlockSpec(memory_space=pltpu.HBM),
        scratch_shapes=[
            pltpu.VMEM((layers * rows, lanes), jnp.float32),
            pltpu.VMEM(params.shape, jnp.float32),
            pltpu.SemaphoreType.DMA((layers,)),
        ],
        compiler_params=pltpu.CompilerParams(vmem_limit_bytes=4 * 2**20),
    )(fragment, params, first_moment, second_moment, new_global, *parts)


def shards(inputs, cotangent, weights, first_moment, second_moment, anchor, momentum, fragment):
    tokens = inputs[0]
    upstream = cotangent[0]
    params = weights[0]
    layers, rows = params.shape[0], params.shape[1]
    model_width = tokens.shape[1]
    groups = lax.axis_size("fsdp")
    replicas = lax.axis_size("rep")
    units = rows * 128 // model_width
    hidden = units * groups // 2
    piece = layers * units
    compact = params.astype(jnp.bfloat16).reshape(piece, 2, model_width // 2)
    compact = compact.transpose(1, 0, 2).reshape(2 * piece, model_width // 2)
    other = swap(params, "rep", 1)
    kept = []

    def stage(blocks):
        kept.append(stage_tokens(tokens, blocks))
        return kept[0]

    gathered = gather_blocks(compact, "fsdp", stage, other)
    squares = kept[0]

    sets = output_sets(groups)
    if piece == ROWS:
        outs = adapter_grads(tokens, upstream, squares, gathered, units, sets)
    else:
        merged = ROWS // piece
        blocks = {k: array[place] for ks, array in gathered for place, k in enumerate(ks)}
        blocks = jnp.stack([blocks[k] for k in range(groups)])
        blocks = blocks.reshape(groups // merged, merged, 2, piece, model_width // 2)
        blocks = blocks.transpose(0, 2, 1, 3, 4).reshape(groups // merged, 2 * ROWS, model_width // 2)
        every = list(range(groups // merged))
        (both,) = adapter_grads(tokens, upstream, squares, [(every, blocks)], units, [every])
        both = both.reshape(groups // merged, 2, merged, piece, model_width // 2)
        both = both.transpose(0, 2, 1, 3, 4).reshape(groups, 2 * piece, model_width // 2)
        outs = [jnp.stack([both[k] for k in ks]) for ks in sets]
    summed, late = reduce_blocks(outs, "fsdp")

    total = fragment_delta(fragment, params, after(other, late), anchor)
    step = 2
    while step < replicas:
        total = total + swap(total, "rep", step)
        step *= 2
    mean_delta = total / replicas
    new_velocity = outer_beta * momentum + mean_delta
    new_global = anchor - outer_rate * (mean_delta + outer_beta * new_velocity)
    scales = (model_width ** (-0.5), hidden ** (-0.5))
    merged = adam_step(
        fragment, params, first_moment[0], second_moment[0], new_global, [summed], tokens.shape[0] * groups, scales
    )
    return (merged[None], new_global, new_velocity)


def solution(mesh):
    placed = (
        P("rep", "fsdp", None),
        P("rep", "fsdp", None),
        P("rep", None, "fsdp", None),
        P("rep", None, "fsdp", None),
        P("rep", None, "fsdp", None),
        P("fsdp", None),
        P("fsdp", None),
        P(),
    )
    return jax.shard_map(
        shards,
        mesh=mesh,
        in_specs=placed,
        out_specs=(P("rep", None, "fsdp", None), P("fsdp", None), P("fsdp", None)),
        check_vma=False,
    )
```
